256 devices in a mesh: rows: 16 (over x, z_lo, core), cols: 16 (over z_hi, y).
Axes of the slice: x: 4, y: 4, z: 8 (z_hi: 4, z_lo: 2; z = z_hi * 2 + z_lo), core: 2. Of those that a mesh axis runs over, the one named last changes fastest.
Arguments:
- counts: int32 [32768, 16384], P('rows', 'cols'), may hold values from 0 to 256, as said below
- row_sums: int32 [32768], P('rows'), may hold values from 30000 to 999999
- col_sums: int32 [16384], P('cols'), may hold values from 30000 to 999999
- log_total: float32 [1], replicated, may hold values from 22 to 26
- row_emb: bfloat16 [32768, 256], P(('rows', 'cols')), may hold values from -1.5 to 1.5
- col_emb: bfloat16 [16384, 256], P(('cols', 'rows')), may hold values from -1.5 to 1.5
Outputs:
- row_grad: float32 [32768, 256], P(('rows', 'cols'))
- col_grad: float32 [16384, 256], P(('cols', 'rows'))
The draws below stay inside these ranges and needn't reach their ends.
Inputs may be any that keep to these rules, and one draw needn't show every extreme that they name: `counts`: about five cells in fourteen are zero.
All inputs are finite; a program needn't handle non-finite values.
Results may differ from the reference program's by a relative error of at most 0.0013.
Values may be sent and summed in bfloat16 or wider, within the bound.
A program may use at most 64 MiB of HBM per device.

```python
import math
import jax
import jax.numpy as jnp
from jax import lax

D = 256
TILE = 1024
NR = 32768
NC = 16384
N_ROWS = 16


def draw_counts(key, part):
    key = jax.random.fold_in(key, 11)
    level_key, value_key = jax.random.split(key)
    level = jax.random.randint(level_key, (NR, NC), 0, 14)
    width = jnp.left_shift(jnp.int32(1), jnp.maximum(level - 5, 0))
    raw = jax.random.randint(value_key, (NR, NC), 0, 1073741824)
    return jnp.where(level >= 5, raw % width + 1, 0).astype(jnp.int32)


def touch_ends(drawn, key, least, top_value):
    longest = drawn.shape.index(max(drawn.shape))
    spots = []
    for shift in (0, 1):
        where = [jax.random.randint(jax.random.fold_in(key, axis), (), 0, length) for axis, length in enumerate(drawn.shape)]
        where[longest] = (where[longest] + shift) % drawn.shape[longest]
        spots.append(tuple(where))
    return drawn.at[spots[0]].set(least).at[spots[1]].set(top_value)


def level_of(key, shape, cuts, low, largest):
    loudness, own = 1.0, jax.random.fold_in(key, 6)
    for dim, shards_of in cuts:
        steps = jnp.exp(jax.random.uniform(jax.random.fold_in(own, dim), (shards_of,), jnp.float32, low / len(cuts), largest / len(cuts)))
        loudness = loudness * jnp.repeat(steps, shape[dim] // shards_of).reshape([-1 if axis == dim else 1 for axis in range(len(shape))])
    return loudness


def normal_values(stream_key, extent, spread, most, cuts=(), kind=jnp.bfloat16):
    result = jax.random.normal(stream_key, extent, jnp.float32) * spread
    if len(cuts) > 0:
        result = level_of(stream_key, extent, cuts, -0.22, 0.18) * result
    return jnp.clip(result, min=-most, max=most).astype(kind)


def setup_inputs(seed: int = 0) -> dict:
    seeds = jax.random.split(jax.random.key(seed), 7)
    counts = draw_counts(jax.random.fold_in(seeds[6], 71), 0)
    row_sums = touch_ends(jax.random.randint(seeds[1], (NR,), 30000, 1000000), jax.random.fold_in(seeds[1], 1), 30000, 999999).astype(jnp.int32)
    col_sums = touch_ends(jax.random.randint(seeds[2], (NC,), 30000, 1000000), jax.random.fold_in(seeds[2], 1), 30000, 999999).astype(jnp.int32)
    log_total = jnp.clip(jax.random.uniform(seeds[3], (1,), jnp.float32, 22.0, 26.0), 22.0, 26.0)
    row_emb = normal_values(seeds[4], (NR, D), 0.25, 1.5, ((0, 256),))
    col_emb = normal_values(seeds[5], (NC, D), 0.25, 1.5, ((0, 256),))
    return {"counts": counts, "row_sums": row_sums, "col_sums": col_sums, "log_total": log_total, "row_emb": row_emb, "col_emb": col_emb}


def cell_grads(counts, scores, row_logs, col_logs, log_total, scale):
    count_f = counts.astype(jnp.float32)
    pmi = log_total - row_logs[:, None] - col_logs[None, :]
    conf = 0.1 + 0.25 * jnp.sqrt(count_f)
    fitted = conf * (scores - jnp.log(jnp.maximum(count_f, 1.0)) - pmi)
    hinge = jax.nn.sigmoid(scores - pmi)
    return (jnp.where(counts > 0, fitted, hinge) * scale).astype(jnp.bfloat16)

def reference(counts, row_sums, col_sums, log_total, row_emb, col_emb):
    block = 2 * TILE
    scale = 1.0 / math.sqrt(NC)
    cnt = counts.reshape(N_ROWS, block, NC)
    rws = row_emb.reshape(N_ROWS, block, D)
    rsm = row_sums.reshape(N_ROWS, block)
    col_logs = jnp.log(col_sums.astype(jnp.float32))

    def one_block(carry, inputs):
        cblock, rblock, sblock = inputs
        scores = jnp.dot(rblock, col_emb.T, preferred_element_type=jnp.float32)
        grads = cell_grads(cblock, scores, jnp.log(sblock.astype(jnp.float32)), col_logs, log_total[0], scale)
        row_part = jnp.dot(grads, col_emb, preferred_element_type=jnp.float32)
        col_part = jnp.dot(grads.T, rblock, preferred_element_type=jnp.float32)
        return (carry + col_part, row_part)
    start = jnp.zeros((NC, D), jnp.float32)
    col_grad, row_parts = lax.scan(one_block, start, (cnt, rws, rsm))
    return (row_parts.reshape(NR, D), col_grad)
```

```python
import math

import jax
import jax.numpy as jnp
from jax import lax
from jax.experimental import pallas as pl
from jax.experimental.pallas import tpu as pltpu
from jax.sharding import PartitionSpec as P

MESH = pl.DeviceIdType.MESH
D = 256
CHUNK = 128
PART = 64
SET = 4 * CHUNK
TILE = 4 * PART
LEVELS = 32000.0
STEPS = 8.0
ORDER = (1, 3, 2)


def encode(ref, value):
    rows = value.shape[0]
    top = jnp.max(jnp.abs(value), axis=0, keepdims=True)
    power = jnp.ceil(jnp.log(jnp.maximum(top, 1e-33)) * (STEPS / math.log(2.0)))
    inverse = jnp.exp(power * (-math.log(2.0) / STEPS)) * LEVELS
    ref[0:rows, :] = jnp.round(value * inverse).astype(jnp.int32).astype(jnp.int16)
    ref[rows : rows + 16, :] = (
        jnp.broadcast_to(power, (16, value.shape[1])).astype(jnp.int32).astype(jnp.int16)
    )


def decode(ref, rows):
    power = ref[rows : rows + 16, :].astype(jnp.int32).astype(jnp.float32)[0:1]
    scale = jnp.exp(power * (math.log(2.0) / STEPS)) * (1.0 / LEVELS)
    return ref[0:rows, :].astype(jnp.int32).astype(jnp.float32) * scale


def cell_grads(counts, scores, scale):
    at_least_one = jnp.maximum(counts.astype(jnp.float32), 1.0)
    root = at_least_one * lax.rsqrt(at_least_one)
    conf = (0.1 * scale) + (0.25 * scale) * root
    fitted = conf * (scores - jnp.log(at_least_one))
    hinge = (0.5 * scale) + (0.5 * scale) * jnp.tanh(0.5 * scores)
    return jnp.where(counts > 0, fitted, hinge).astype(jnp.bfloat16)


def kernel(
    scale,
    counts_hbm, row_sums_hbm, col_sums_hbm, log_total, row_emb, col_emb,
    row_out, col_out,
    counts, row_sums, col_sums, rows, cols, row_bias, col_bias,
    kept, row_total, col_total,
    y_out, y_in, z_out, z_in, c_out, c_in, x_out, x_in,
    local_sem, counts_sem,
    gz_send, gz_recv, gy_send, gy_recv, gx_send, gx_recv, gc_send, gc_recv,
    ry_send, ry_recv, rz_send, rz_recv, rc_send, rc_recv, rx_send, rx_recv,
):
    r, k = lax.axis_index("rows"), lax.axis_index("cols")
    x, zl, c = r // 4, (r // 2) % 2, r % 2
    zh, y = k // 4, k % 4

    def col_peer(dz, dy):
        return (r, lax.rem(zh + dz, 4) * 4 + lax.rem(y + dy, 4))

    def row_peer(dx, dl, dc):
        return (lax.rem(x + dx, 4) * 4 + lax.rem(zl + dl, 2) * 2 + lax.rem(c + dc, 2), k)

    def chunk_at(z, yy):
        return pl.ds(pl.multiple_of((z * 4 + yy) * CHUNK, CHUNK), CHUNK)

    def part_at(index):
        return pl.ds(pl.multiple_of(index * PART, PART), PART)

    def remote(src, dst, send, recv, to):
        return pltpu.make_async_remote_copy(
            src_ref=src, dst_ref=dst, send_sem=send, recv_sem=recv, device_id=to, device_id_type=MESH
        )

    same_core = [(dx, dl) for dx in range(4) for dl in range(2) if dx or dl]

    own_rows, own_cols = chunk_at(zh, y), part_at(r)
    local = [
        pltpu.make_async_copy(row_emb, rows.at[own_rows], local_sem.at[0]),
        pltpu.make_async_copy(col_emb, cols.at[own_cols], local_sem.at[1]),
        pltpu.make_async_copy(row_sums_hbm, row_sums, local_sem.at[2]),
        pltpu.make_async_copy(col_sums_hbm, col_sums, local_sem.at[3]),
    ]
    for copy in local:
        copy.start()
    barrier = pltpu.get_barrier_semaphore()
    peers = [col_peer(d, 0) for d in (1, 2, 3)] + [col_peer(0, d) for d in (1, 2, 3)]
    peers += [row_peer(dx, dl, 0) for dx, dl in same_core] + [row_peer(0, 0, 1)]
    for peer in peers:
        pl.semaphore_signal(barrier, inc=1, device_id=peer, device_id_type=MESH)
    counts_in = []
    for n in range(4):
        at = pl.ds(n * SET, SET)
        counts_in.append(pltpu.make_async_copy(counts_hbm.at[at], counts.at[at], counts_sem.at[n]))
        counts_in[-1].start()
    for copy in local:
        copy.wait()
    pl.semaphore_wait(barrier, len(peers))

    sends = []

    def go(copy):
        copy.start()
        sends.append(copy)
        return copy

    for d in ORDER:
        go(remote(rows.at[own_rows], rows.at[own_rows], gz_send.at[d], gz_recv.at[d], col_peer(d, 0)))
    for e in (1, 3, 2):
        go(remote(rows.at[own_rows], rows.at[own_rows], gy_send.at[0, e], gy_recv.at[0, e], col_peer(0, e)))
    for n, (dx, dl) in enumerate(same_core):
        go(remote(cols.at[own_cols], cols.at[own_cols], gx_send.at[n], gx_recv.at[n], row_peer(dx, dl, 0)))
    go(remote(cols.at[own_cols], cols.at[own_cols], gc_send.at[7], gc_recv.at[7], row_peer(0, 0, 1)))

    row_logs = jnp.log(row_sums[...].astype(jnp.float32)) - log_total[0]
    for n in range(16):
        square = jnp.broadcast_to(row_logs[n : n + 1, :], (CHUNK, CHUNK))
        row_bias[n * CHUNK : (n + 1) * CHUNK, :] = square.T
    col_logs = jnp.log(col_sums[...].astype(jnp.float32))
    for t in range(4):
        both = [jnp.broadcast_to(col_logs[2 * t + h : 2 * t + h + 1, :], (8, CHUNK)) for h in (0, 1)]
        col_bias[t] = jnp.concatenate(both, axis=1)
    col_total[...] = jnp.zeros_like(col_total)

    def forward_rows(d):
        z = lax.rem(zh + 4 - d, 4)
        at = chunk_at(z, y)
        remote(rows.at[at], rows.at[at], gz_send.at[d], gz_recv.at[d], col_peer(d, 0)).wait_recv()
        for e in (1, 3, 2):
            go(remote(rows.at[at], rows.at[at], gy_send.at[d, e], gy_recv.at[d, e], col_peer(0, e)))

    def forward_cols(n):
        dx, dl = same_core[n]
        origin = lax.rem(x + 4 - dx, 4) * 4 + lax.rem(zl + dl, 2) * 2 + c
        at = part_at(origin)
        remote(cols.at[at], cols.at[at], gx_send.at[n], gx_recv.at[n], row_peer(dx, dl, 0)).wait_recv()
        go(remote(cols.at[at], cols.at[at], gc_send.at[n], gc_recv.at[n], row_peer(0, 0, 1)))

    forward_rows(1)
    forward_rows(3)
    for n in range(7):
        forward_cols(n)
    forward_rows(2)
    for n in range(8):
        dx, dl = same_core[n] if n < 7 else (0, 0)
        origin = lax.rem(x + 4 - dx, 4) * 4 + lax.rem(zl + dl, 2) * 2 + (1 - c)
        at = part_at(origin)
        remote(cols.at[at], cols.at[at], gc_send.at[n], gc_recv.at[n], row_peer(0, 0, 1)).wait_recv()
    for copy in counts_in:
        copy.wait()

    def wait_set(d):
        z = lax.rem(zh + 4 - d, 4)
        for e in (1, 3, 2):
            at = chunk_at(z, lax.rem(y + 4 - e, 4))
            remote(rows.at[at], rows.at[at], gy_send.at[d, e], gy_recv.at[d, e], col_peer(0, e)).wait_recv()

    def grads_of(at, tile, width):
        col_at = pl.ds(pl.multiple_of(tile * TILE, TILE), width)
        some = cols[col_at, :]
        scores = lax.dot_general(
            rows[at, :], some, (((1,), (1,)), ((), ())), preferred_element_type=jnp.float32
        )
        bias = jnp.concatenate([row_bias[at, :]] * (width // CHUNK), axis=1)
        side = jnp.concatenate([col_bias[tile + n, 0:1, :] for n in range(width // TILE)], axis=1)
        return cell_grads(counts[at, col_at], scores + bias + side, scale), some, col_at

    def send_rows(d, total):
        for e in (2, 1, 3):
            encode(y_out.at[d, e - 1], total[pl.ds(pl.multiple_of(lax.rem(y + e, 4) * CHUNK, CHUNK), CHUNK), :])
            remote(y_out.at[d, e - 1], y_in.at[d, e - 1], ry_send.at[d, e], ry_recv.at[d, e], col_peer(0, e)).start()
        kept[d] = total[pl.ds(pl.multiple_of(y * CHUNK, CHUNK), CHUNK), :]

    def sum_rows(d):
        total = kept[d]
        for e in (1, 3, 2):
            remote(y_out.at[d, e - 1], y_in.at[d, e - 1], ry_send.at[d, e], ry_recv.at[d, e], col_peer(0, e)).wait_recv()
            total = total + decode(y_in.at[d, e - 1], CHUNK)
        return total

    def send_z(d):
        encode(z_out.at[d - 1], sum_rows(d))
        go(remote(z_out.at[d - 1], z_in.at[d - 1], rz_send.at[d], rz_recv.at[d], col_peer(4 - d, 0)))

    def one_set(step, _):
        d = lax.rem(1 + 2 * step - 3 * (step // 2), 4)
        z = lax.rem(zh + 4 - d, 4)
        wait_set(d)
        at = pl.ds(pl.multiple_of(z * SET, SET), SET)
        for tile in (0, 2):
            grads, some, col_at = grads_of(at, tile, 2 * TILE)
            part = jnp.dot(grads, some, preferred_element_type=jnp.float32)
            row_total[...] = part if tile == 0 else row_total[...] + part
            col_total[col_at, :] += lax.dot_general(
                grads, rows[at, :], (((0,), (0,)), ((), ())), preferred_element_type=jnp.float32
            )
        send_rows(d, row_total)
        return 0

    lax.fori_loop(0, 3, one_set, 0)
    send_z(1)

    wait_set(0)
    at = pl.ds(pl.multiple_of(zh * SET, SET), SET)
    for n in range(4):
        tile = lax.rem(x + 1 + n, 4)
        grads, some, col_at = grads_of(at, tile, TILE)
        part = jnp.dot(grads, some, preferred_element_type=jnp.float32)
        row_total[...] = part if n == 0 else row_total[...] + part
        col_total[col_at, :] += lax.dot_general(
            grads, rows[at, :], (((0,), (0,)), ((), ())), preferred_element_type=jnp.float32
        )
        theirs = [col_total[part_at(tile * 4 + 2 * h + 1 - c), :] for h in (0, 1)]
        encode(c_out.at[n], jnp.concatenate(theirs, axis=0))
        go(remote(c_out.at[n], c_in.at[n], rc_send.at[n], rc_recv.at[n], row_peer(0, 0, 1)))
    send_rows(0, row_total)


    own_cols_sum = None
    for n in range(4):
        tile = lax.rem(x + 1 + n, 4)
        remote(c_out.at[n], c_in.at[n], rc_send.at[n], rc_recv.at[n], row_peer(0, 0, 1)).wait_recv()
        mine = [col_total[part_at(tile * 4 + 2 * h + c), :] for h in (0, 1)]
        both = decode(c_in.at[n], 2 * PART) + jnp.concatenate(mine, axis=0)
        here = jnp.where(zl == 0, both[0:PART], both[PART:])
        there = jnp.where(zl == 0, both[PART:], both[0:PART])
        slot = 2 * n
        if n < 3:
            encode(x_out.at[slot + 1], here)
            go(remote(x_out.at[slot + 1], x_in.at[slot + 1], rx_send.at[slot + 1], rx_recv.at[slot + 1], row_peer(n + 1, 0, 0)))
        else:
            own_cols_sum = here
        encode(x_out.at[slot], there)
        go(remote(x_out.at[slot], x_in.at[slot], rx_send.at[slot], rx_recv.at[slot], row_peer((n + 1) % 4, 1, 0)))

    send_z(3)
    send_z(2)
    row_sum = sum_rows(0)
    for slot in range(7):
        n, dl = slot // 2, 1 - slot % 2
        remote(x_out.at[slot], x_in.at[slot], rx_send.at[slot], rx_recv.at[slot], row_peer((n + 1) % 4, dl, 0)).wait_recv()
        own_cols_sum = own_cols_sum + decode(x_in.at[slot], PART)
    col_out[...] = own_cols_sum
    for d in ORDER:
        remote(z_out.at[d - 1], z_in.at[d - 1], rz_send.at[d], rz_recv.at[d], col_peer(4 - d, 0)).wait_recv()
        row_sum = row_sum + decode(z_in.at[d - 1], CHUNK)
    row_out[...] = row_sum

    for copy in sends:
        copy.wait_send()
    for d in range(4):
        for e in (1, 2, 3):
            remote(y_out.at[d, e - 1], y_in.at[d, e - 1], ry_send.at[d, e], ry_recv.at[d, e], col_peer(0, e)).wait_send()


def shards(counts, row_sums, col_sums, log_total, row_emb, col_emb):
    n_cols = lax.axis_size("cols")
    scale = 1.0 / math.sqrt(col_sums.shape[0] * n_cols)
    dma = pltpu.SemaphoreType.DMA

    def body(*refs):
        kernel(scale, *refs)

    anywhere = pl.BlockSpec(memory_space=pl.ANY)
    vmem = pl.BlockSpec(memory_space=pltpu.VMEM)
    message = (CHUNK + 16, D)
    return pl.pallas_call(
        body,
        name="swivel",
        out_shape=(
            jax.ShapeDtypeStruct((CHUNK, D), jnp.float32),
            jax.ShapeDtypeStruct((PART, D), jnp.float32),
        ),
        in_specs=[anywhere] * 3 + [pl.BlockSpec(memory_space=pltpu.SMEM)] + [anywhere] * 2,
        out_specs=(vmem, vmem),
        scratch_shapes=[
            pltpu.VMEM(counts.shape, jnp.int32),
            pltpu.VMEM((16, CHUNK), jnp.int32),
            pltpu.VMEM((8, CHUNK), jnp.int32),
            pltpu.VMEM((16 * CHUNK, D), jnp.bfloat16),
            pltpu.VMEM((16 * PART, D), jnp.bfloat16),
            pltpu.VMEM((16 * CHUNK, CHUNK), jnp.float32),
            pltpu.VMEM((4, 8, TILE), jnp.float32),
            pltpu.VMEM((4, CHUNK, D), jnp.float32),
            pltpu.VMEM((SET, D), jnp.float32),
            pltpu.VMEM((16 * PART, D), jnp.float32),
            pltpu.VMEM((4, 3) + message, jnp.int16),
            pltpu.VMEM((4, 3) + message, jnp.int16),
            pltpu.VMEM((3,) + message, jnp.int16),
            pltpu.VMEM((3,) + message, jnp.int16),
            pltpu.VMEM((4,) + message, jnp.int16),
            pltpu.VMEM((4,) + message, jnp.int16),
            pltpu.VMEM((7, PART + 16, D), jnp.int16),
            pltpu.VMEM((7, PART + 16, D), jnp.int16),
            dma((4,)),
            dma((4,)),
            dma((4,)), dma((4,)),
            dma((4, 4)), dma((4, 4)),
            dma((7,)), dma((7,)),
            dma((8,)), dma((8,)),
            dma((4, 4)), dma((4, 4)),
            dma((4,)), dma((4,)),
            dma((4,)), dma((4,)),
            dma((7,)), dma((7,)),
        ],
        compiler_params=pltpu.CompilerParams(
            collective_id=0, has_side_effects=True, vmem_limit_bytes=48 << 20
        ),
        cost_estimate=pl.CostEstimate(
            flops=6 * 2048 * 1024 * 256, bytes_accessed=9 << 20, transcendentals=3 * 2048 * 1024
        ),
    )(counts, row_sums.reshape(16, CHUNK), col_sums.reshape(8, CHUNK), log_total, row_emb, col_emb)


def solution(mesh):
    in_specs = (
        P("rows", "cols"),
        P("rows"),
        P("cols"),
        P(),
        P(("rows", "cols"), None),
        P(("cols", "rows"), None),
    )
    out_specs = (P(("rows", "cols"), None), P(("cols", "rows"), None))
    return jax.shard_map(shards, mesh=mesh, in_specs=in_specs, out_specs=out_specs, check_vma=False)
```

```python
import math

import jax
import jax.numpy as jnp
from jax import lax
from jax.experimental import pallas as pl
from jax.experimental.pallas import tpu as pltpu
from jax.sharding import PartitionSpec as P

MESH = pl.DeviceIdType.MESH
D = 256
CHUNK = 128
PART = 64
SET = 4 * CHUNK
TILE = 4 * PART
LEVELS = 32000.0
STEPS = 8.0
COLUMN_ORDER = (0, 1, 5, 3, 2, 6, 4)
SETS = (1, 2, 3)


def encode(ref, value):
    rows = value.shape[0]
    top = jnp.max(jnp.abs(value), axis=0, keepdims=True)
    power = jnp.ceil(jnp.log(jnp.maximum(top, 1e-33)) * (STEPS / math.log(2.0)))
    inverse = jnp.exp(power * (-math.log(2.0) / STEPS)) * LEVELS
    ref[0:rows, :] = jnp.round(value * inverse).astype(jnp.int32).astype(jnp.int16)
    ref[rows : rows + 16, :] = (
        jnp.broadcast_to(power, (16, value.shape[1])).astype(jnp.int32).astype(jnp.int16)
    )


def decode(ref, rows):
    power = ref[rows : rows + 16, :].astype(jnp.int32).astype(jnp.float32)[0:1]
    scale = jnp.exp(power * (math.log(2.0) / STEPS)) * (1.0 / LEVELS)
    return ref[0:rows, :].astype(jnp.int32).astype(jnp.float32) * scale


def cell_grads(counts, scores, scale):
    at_least_one = jnp.maximum(counts.astype(jnp.float32), 1.0)
    root = at_least_one * lax.rsqrt(at_least_one)
    conf = (0.1 * scale) + (0.25 * scale) * root
    fitted = conf * (scores - jnp.log(at_least_one))
    hinge = (0.5 * scale) + (0.5 * scale) * jnp.tanh(0.5 * scores)
    return jnp.where(counts > 0, fitted, hinge).astype(jnp.bfloat16)


def kernel(
    scale,
    counts_hbm, row_sums_hbm, col_sums_hbm, log_total, row_emb, col_emb,
    row_out, col_out,
    counts, row_sums, col_sums, rows, cols, row_bias, col_bias,
    kept, far, row_total, col_total,
    y_out, y_in, b_in, z_out, z_in, c_out, c_in, x_out, x_in, l_out, l_in,
    local_sem, counts_sem,
    gz_send, gz_recv, gy_send, gy_recv, gx_send, gx_recv, gc_send, gc_recv,
    ry_send, ry_recv, rb_send, rb_recv, rz_send, rz_recv, rc_send, rc_recv, rx_send, rx_recv, rl_send, rl_recv,
):
    r, k = lax.axis_index("rows"), lax.axis_index("cols")
    x, zl, c = r // 4, (r // 2) % 2, r % 2
    zh, y = k // 4, k % 4

    def col_peer(dz, dy):
        return (r, lax.rem(zh + dz, 4) * 4 + lax.rem(y + dy, 4))

    def row_peer(dx, dl, dc):
        return (lax.rem(x + dx, 4) * 4 + lax.rem(zl + dl, 2) * 2 + lax.rem(c + dc, 2), k)

    def chunk_at(z, yy):
        return pl.ds(pl.multiple_of((z * 4 + yy) * CHUNK, CHUNK), CHUNK)

    def part_at(index):
        return pl.ds(pl.multiple_of(index * PART, PART), PART)

    def remote(src, dst, send, recv, to):
        return pltpu.make_async_remote_copy(
            src_ref=src, dst_ref=dst, send_sem=send, recv_sem=recv, device_id=to, device_id_type=MESH
        )

    same_core = [(dx, dl) for dx in range(4) for dl in range(2) if dx or dl]

    own_rows, own_cols = chunk_at(zh, y), part_at(r)
    local = [
        pltpu.make_async_copy(row_emb, rows.at[own_rows], local_sem.at[0]),
        pltpu.make_async_copy(col_emb, cols.at[own_cols], local_sem.at[1]),
        pltpu.make_async_copy(row_sums_hbm, row_sums, local_sem.at[2]),
        pltpu.make_async_copy(col_sums_hbm, col_sums, local_sem.at[3]),
    ]
    for copy in local:
        copy.start()
    barrier = pltpu.get_barrier_semaphore()
    peers = [col_peer(d, 0) for d in (1, 2, 3)] + [col_peer(0, d) for d in (1, 2, 3)]
    peers += [row_peer(dx, dl, 0) for dx, dl in same_core] + [row_peer(0, 0, 1)]
    for peer in peers:
        pl.semaphore_signal(barrier, inc=1, device_id=peer, device_id_type=MESH)
    counts_in = []
    for n in range(4):
        at = pl.ds(n * SET, SET)
        counts_in.append(pltpu.make_async_copy(counts_hbm.at[at], counts.at[at], counts_sem.at[n]))
        counts_in[-1].start()
    for copy in local:
        copy.wait()
    pl.semaphore_wait(barrier, len(peers))

    sends = []

    def go(copy):
        copy.start()
        sends.append(copy)
        return copy

    def z_gather(d):
        at = chunk_at(lax.rem(zh + 4 - d, 4), y)
        return remote(rows.at[at], rows.at[at], gz_send.at[d], gz_recv.at[d], col_peer(d, 0))

    def send_cols(dx, dl):
        at, n = part_at(x * 4 + lax.rem(zl + dl, 2) * 2 + c), 2 * dx + dl - 1
        go(remote(cols.at[at], cols.at[at], gx_send.at[n], gx_recv.at[n], row_peer(dx, 0, 0)))

    def send_own_rows(d):
        go(remote(rows.at[own_rows], rows.at[own_rows], gz_send.at[d], gz_recv.at[d], col_peer(d, 0)))

    send_own_rows(1)
    send_own_rows(3)
    go(remote(cols.at[own_cols], cols.at[own_cols], gc_send.at[7], gc_recv.at[7], row_peer(0, 0, 1)))
    go(remote(cols.at[own_cols], cols.at[own_cols], gx_send.at[0], gx_recv.at[0], row_peer(0, 1, 0)))
    for dx in (1, 3, 2):
        send_cols(dx, 0)
    for e in (1, 3, 2):
        go(remote(rows.at[own_rows], rows.at[own_rows], gy_send.at[0, e], gy_recv.at[0, e], col_peer(0, e)))
    send_own_rows(2)

    row_logs = jnp.log(row_sums[...].astype(jnp.float32)) - log_total[0]
    for n in range(16):
        square = jnp.broadcast_to(row_logs[n : n + 1, :], (CHUNK, CHUNK))
        row_bias[n * CHUNK : (n + 1) * CHUNK, :] = square.T
    col_logs = jnp.log(col_sums[...].astype(jnp.float32))
    for t in range(4):
        both = [jnp.broadcast_to(col_logs[2 * t + h : 2 * t + h + 1, :], (8, CHUNK)) for h in (0, 1)]
        col_bias[t] = jnp.concatenate(both, axis=1)

    def forward_rows(d):
        at = chunk_at(lax.rem(zh + 4 - d, 4), y)
        z_gather(d).wait_recv()
        for e in (1, 3, 2):
            go(remote(rows.at[at], rows.at[at], gy_send.at[d, e], gy_recv.at[d, e], col_peer(0, e)))

    def y_gather(d, e):
        at = chunk_at(lax.rem(zh + 4 - d, 4), lax.rem(y + 4 - e, 4))
        return remote(rows.at[at], rows.at[at], gy_send.at[d, e], gy_recv.at[d, e], col_peer(0, e))

    def origin(dx, dl, core):
        return part_at(lax.rem(x + 4 - dx, 4) * 4 + lax.rem(zl + dl, 2) * 2 + core)

    def forward_cols(n):
        dx, dl = same_core[n]
        at = origin(dx, dl, c)
        remote(cols.at[at], cols.at[at], gx_send.at[n], gx_recv.at[n], row_peer(dx, dl, 0)).wait_recv()
        go(remote(cols.at[at], cols.at[at], gc_send.at[n], gc_recv.at[n], row_peer(0, 0, 1)))
        if n == 0:
            for peer in (1, 3, 2):
                send_cols(peer, 1)

    def wait_cols(dx):
        for dl in (0, 1):
            n = lax.rem(2 * dx + dl + 7, 8)
            at = origin(dx, dl, 1 - c)
            remote(cols.at[at], cols.at[at], gc_send.at[n], gc_recv.at[n], row_peer(0, 0, 1)).wait_recv()

    def wait_set(d):
        for e in (1, 3, 2):
            y_gather(d, e).wait_recv()

    def grads_of(at, tile, width):
        col_at = pl.ds(pl.multiple_of(tile * TILE, TILE), width)
        some = cols[col_at, :]
        scores = lax.dot_general(
            rows[at, :], some, (((1,), (1,)), ((), ())), preferred_element_type=jnp.float32
        )
        bias = jnp.concatenate([row_bias[at, :]] * (width // CHUNK), axis=1)
        side = jnp.concatenate([col_bias[tile + n, 0:1, :] for n in range(width // TILE)], axis=1)
        return cell_grads(counts[at, col_at], scores + bias + side, scale), some, col_at

    def tile_step(at, tile, width, first_rows, first_cols):
        grads, some, col_at = grads_of(at, tile, width)
        part = jnp.dot(grads, some, preferred_element_type=jnp.float32)
        row_total[...] = part if first_rows else row_total[...] + part
        part = lax.dot_general(
            grads, rows[at, :], (((0,), (0,)), ((), ())), preferred_element_type=jnp.float32
        )
        col_total[col_at, :] = part if first_cols else col_total[col_at, :] + part

    def set_at(d):
        return pl.ds(pl.multiple_of(lax.rem(zh + 4 - d, 4) * SET, SET), SET)

    def y_message(d, e):
        return remote(
            y_out.at[d, e - 1], y_in.at[d, e - 1], ry_send.at[d, e], ry_recv.at[d, e], col_peer(0, e)
        )

    def far_message(d):
        n = d // 2
        return remote(y_out.at[d, 1], b_in.at[n], rb_send.at[n], rb_recv.at[n], col_peer(4 - d, 0))

    def z_message(d):
        return remote(z_out.at[d - 1], z_in.at[d - 1], rz_send.at[d], rz_recv.at[d], col_peer(4 - d, 0))

    def peer_rows(e):
        return row_total[pl.ds(pl.multiple_of(lax.rem(y + e, 4) * CHUNK, CHUNK), CHUNK), :]

    def encode_rows(d):
        if d == 0:
            far[...] = peer_rows(2)
        else:
            encode(y_out.at[d, 1], peer_rows(2))
        encode(y_out.at[d, 0], peer_rows(1))
        encode(y_out.at[d, 2], peer_rows(3))
        kept[d] = peer_rows(0)

    def send_rows(d):
        if d % 2:
            far_message(d).start()
        elif d:
            y_message(d, 2).start()
        y_message(d, 1).start()
        y_message(d, 3).start()

    def send_far():
        for d in (1, 3):
            far_message(d).wait_recv()
        encode(y_out.at[0, 1], far[...] + decode(b_in.at[0], CHUNK) + decode(b_in.at[1], CHUNK))
        y_message(0, 2).start()

    def sum_rows(d):
        hops = (1, 3) if d % 2 else (1, 3, 2)
        total = kept[d]
        for e in hops:
            y_message(d, e).wait_recv()
        for e in hops:
            total = total + decode(y_in.at[d, e - 1], CHUNK)
        return total

    def send_z(d):
        encode(z_out.at[d - 1], sum_rows(d))
        z_message(d).start()

    odd, pair = x % 2, x // 2
    forward_cols(0)
    forward_rows(1)
    forward_rows(3)
    for n in COLUMN_ORDER[1:]:
        forward_cols(n)
    wait_set(0)
    for copy in counts_in:
        copy.wait()
    wait_cols(0)
    wait_cols(3 - 2 * odd)
    tile_step(set_at(0), 2 * pair, 2 * TILE, True, True)
    wait_cols(2)
    wait_cols(1 + 2 * odd)
    forward_rows(2)
    tile_step(set_at(0), 2 - 2 * pair, 2 * TILE, False, True)
    encode_rows(0)

    for d in SETS[:2]:
        wait_set(d)
        for tile in (0, 2):
            tile_step(set_at(d), tile, 2 * TILE, tile == 0, False)
        encode_rows(d)
        send_rows(d)
        if d == SETS[0]:
            send_rows(0)

    def core_message(n):
        return remote(c_out.at[n], c_in.at[n], rc_send.at[n], rc_recv.at[n], row_peer(0, 0, 1))

    def x_message(n):
        return remote(x_out.at[n], x_in.at[n], rx_send.at[n], rx_recv.at[n], row_peer(n + 1, 0, 0))

    def core_rows(n, h, core):
        return part_at(lax.rem(x + 1 + n, 4) * 4 + 2 * h + core)

    def send_core(n):
        theirs = [col_total[core_rows(n, h, 1 - c), :] for h in (0, 1)]
        encode(c_out.at[n], jnp.concatenate(theirs, axis=0))
        core_message(n).start()

    wait_set(SETS[2])
    tile_step(set_at(SETS[2]), 2 - 2 * pair, 2 * TILE, True, False)
    send_core(1)
    send_core(2 - 2 * odd)
    tile_step(set_at(SETS[2]), 2 * pair, 2 * TILE, False, False)
    encode_rows(SETS[2])
    send_rows(SETS[2])
    send_core(2 * odd)
    send_core(3)
    send_z(SETS[0])

    def both_cores(n):
        core_message(n).wait_recv()
        mine = [col_total[core_rows(n, h, c), :] for h in (0, 1)]
        return decode(c_in.at[n], 2 * PART) + jnp.concatenate(mine, axis=0)

    for n in (1, 2 - 2 * odd, 2 * odd):
        encode(x_out.at[n], both_cores(n))
        x_message(n).start()
    both = both_cores(3)

    send_z(SETS[1])
    send_far()
    send_z(SETS[2])
    for n in range(3):
        x_message(n).wait_recv()
        both = both + decode(x_in.at[n], 2 * PART)
    here = jnp.where(zl == 0, both[0:PART], both[PART:])
    encode(l_out, jnp.where(zl == 0, both[PART:], both[0:PART]))
    l_message = go(remote(l_out, l_in, rl_send, rl_recv, row_peer(0, 1, 0)))
    row_sum = sum_rows(0)

    for copy in sends:
        copy.wait_send()
    for d in (0, 1, 2, 3):
        for e in (1, 3) if d % 2 else (1, 2, 3):
            y_message(d, e).wait_send()
    for d in (1, 3):
        far_message(d).wait_send()
    for n in range(4):
        core_message(n).wait_send()
    for n in range(3):
        x_message(n).wait_send()
    l_message.wait_recv()
    col_out[...] = here + decode(l_in, PART)
    for d in SETS:
        z_message(d).wait_recv()
        row_sum = row_sum + decode(z_in.at[d - 1], CHUNK)
    row_out[...] = row_sum
    for d in SETS:
        z_message(d).wait_send()


def shards(counts, row_sums, col_sums, log_total, row_emb, col_emb):
    n_cols = lax.axis_size("cols")
    scale = 1.0 / math.sqrt(col_sums.shape[0] * n_cols)
    dma = pltpu.SemaphoreType.DMA

    def body(*refs):
        kernel(scale, *refs)

    def hbm(array):
        return pltpu.with_memory_space_constraint(array, pltpu.HBM)

    anywhere = pl.BlockSpec(memory_space=pl.ANY)
    vmem = pl.BlockSpec(memory_space=pltpu.VMEM)
    message = (CHUNK + 16, D)
    return pl.pallas_call(
        body,
        name="swivel",
        out_shape=(
            jax.ShapeDtypeStruct((CHUNK, D), jnp.float32),
            jax.ShapeDtypeStruct((PART, D), jnp.float32),
        ),
        in_specs=[anywhere] * 3 + [pl.BlockSpec(memory_space=pltpu.SMEM)] + [anywhere] * 2,
        out_specs=(vmem, vmem),
        scratch_shapes=[
            pltpu.VMEM(counts.shape, jnp.int32),
            pltpu.VMEM((16, CHUNK), jnp.int32),
            pltpu.VMEM((8, CHUNK), jnp.int32),
            pltpu.VMEM((16 * CHUNK, D), jnp.bfloat16),
            pltpu.VMEM((16 * PART, D), jnp.bfloat16),
            pltpu.VMEM((16 * CHUNK, CHUNK), jnp.float32),
            pltpu.VMEM((4, 8, TILE), jnp.float32),
            pltpu.VMEM((4, CHUNK, D), jnp.float32),
            pltpu.VMEM((CHUNK, D), jnp.float32),
            pltpu.VMEM((SET, D), jnp.float32),
            pltpu.VMEM((16 * PART, D), jnp.float32),
            pltpu.VMEM((4, 3) + message, jnp.int16),
            pltpu.VMEM((4, 3) + message, jnp.int16),
            pltpu.VMEM((2,) + message, jnp.int16),
            pltpu.VMEM((3,) + message, jnp.int16),
            pltpu.VMEM((3,) + message, jnp.int16),
            pltpu.VMEM((4,) + message, jnp.int16),
            pltpu.VMEM((4,) + message, jnp.int16),
            pltpu.VMEM((3,) + message, jnp.int16),
            pltpu.VMEM((3,) + message, jnp.int16),
            pltpu.VMEM((PART + 16, D), jnp.int16),
            pltpu.VMEM((PART + 16, D), jnp.int16),
            dma((4,)),
            dma((4,)),
            dma((4,)), dma((4,)),
            dma((4, 4)), dma((4, 4)),
            dma((7,)), dma((7,)),
            dma((8,)), dma((8,)),
            dma((4, 4)), dma((4, 4)),
            dma((2,)), dma((2,)),
            dma((4,)), dma((4,)),
            dma((4,)), dma((4,)),
            dma((3,)), dma((3,)),
            dma, dma,
        ],
        compiler_params=pltpu.CompilerParams(
            collective_id=0, has_side_effects=True, vmem_limit_bytes=48 << 20
        ),
        cost_estimate=pl.CostEstimate(
            flops=6 * 2048 * 1024 * 256, bytes_accessed=9 << 20, transcendentals=3 * 2048 * 1024
        ),
    )(
        counts, hbm(row_sums.reshape(16, CHUNK)), hbm(col_sums.reshape(8, CHUNK)), log_total, hbm(row_emb), hbm(col_emb)
    )


def solution(mesh):
    in_specs = (
        P("rows", "cols"),
        P("rows"),
        P("cols"),
        P(),
        P(("rows", "cols"), None),
        P(("cols", "rows"), None),
    )
    out_specs = (P(("rows", "cols"), None), P(("cols", "rows"), None))
    return jax.shard_map(shards, mesh=mesh, in_specs=in_specs, out_specs=out_specs, check_vma=False)
```

```python
import math

import jax
import jax.numpy as jnp
from jax import lax
from jax.experimental import pallas as pl
from jax.experimental.pallas import tpu as pltpu
from jax.sharding import PartitionSpec as P

MESH = pl.DeviceIdType.MESH
D = 256
CHUNK = 128
PART = 64
SET = 4 * CHUNK
TILE = 4 * PART
LEVELS = 32000.0
STEPS = 8.0
COLUMN_ORDER = (0, 1, 5, 3, 2, 6, 4)
SETS = (1, 3, 2)


def encode(ref, value):
    rows = value.shape[0]
    top = jnp.max(jnp.abs(value), axis=0, keepdims=True)
    power = jnp.ceil(jnp.log(jnp.maximum(top, 1e-33)) * (STEPS / math.log(2.0)))
    inverse = jnp.exp(power * (-math.log(2.0) / STEPS)) * LEVELS
    ref[0:rows, :] = jnp.round(value * inverse).astype(jnp.int32).astype(jnp.int16)
    ref[rows : rows + 16, :] = (
        jnp.broadcast_to(power, (16, value.shape[1])).astype(jnp.int32).astype(jnp.int16)
    )


def decode(ref, rows):
    power = ref[rows : rows + 16, :].astype(jnp.int32).astype(jnp.float32)[0:1]
    scale = jnp.exp(power * (math.log(2.0) / STEPS)) * (1.0 / LEVELS)
    return ref[0:rows, :].astype(jnp.int32).astype(jnp.float32) * scale


def cell_grads(counts, scores, scale):
    at_least_one = jnp.maximum(counts.astype(jnp.float32), 1.0)
    root = at_least_one * lax.rsqrt(at_least_one)
    conf = (0.1 * scale) + (0.25 * scale) * root
    fitted = conf * (scores - jnp.log(at_least_one))
    hinge = (0.5 * scale) + (0.5 * scale) * jnp.tanh(0.5 * scores)
    return jnp.where(counts > 0, fitted, hinge).astype(jnp.bfloat16)


def kernel(
    scale,
    counts_hbm, row_sums_hbm, col_sums_hbm, log_total, row_emb, col_emb,
    row_out, col_out,
    counts, row_sums, col_sums, rows, cols, row_bias, col_bias,
    kept, far, row_total, col_total,
    y_out, y_in, b_in, z_out, z_in, c_out, c_in, x_out, x_in, l_out, l_in,
    local_sem, counts_sem, sent,
    gz_recv, gs_recv, gf_recv, gx_recv, gc_recv,
    ry_recv, rb_recv, rz_recv, rc_recv, rx_recv, rl_recv,
):
    r, k = lax.axis_index("rows"), lax.axis_index("cols")
    x, zl, c = r // 4, (r // 2) % 2, r % 2
    zh, y = k // 4, k % 4

    def col_peer(dz, dy):
        return (r, lax.rem(zh + dz, 4) * 4 + lax.rem(y + dy, 4))

    def row_peer(dx, dl, dc):
        return (lax.rem(x + dx, 4) * 4 + lax.rem(zl + dl, 2) * 2 + lax.rem(c + dc, 2), k)

    def chunk_at(z, yy):
        return pl.ds(pl.multiple_of((z * 4 + yy) * CHUNK, CHUNK), CHUNK)

    def part_at(index):
        return pl.ds(pl.multiple_of(index * PART, PART), PART)

    def remote(src, dst, send, recv, to):
        return pltpu.make_async_remote_copy(
            src_ref=src, dst_ref=dst, send_sem=send, recv_sem=recv, device_id=to, device_id_type=MESH
        )

    same_core = [(dx, dl) for dx in range(4) for dl in range(2) if dx or dl]

    own_rows, own_cols = chunk_at(zh, y), part_at(r)
    local = [
        pltpu.make_async_copy(row_emb, rows.at[own_rows], local_sem.at[0]),
        pltpu.make_async_copy(col_emb, cols.at[own_cols], local_sem.at[1]),
        pltpu.make_async_copy(row_sums_hbm, row_sums, local_sem.at[2]),
        pltpu.make_async_copy(col_sums_hbm, col_sums, local_sem.at[3]),
    ]
    for copy in local:
        copy.start()
    barrier = pltpu.get_barrier_semaphore()
    peers = [col_peer(d, 0) for d in (1, 2, 3)] + [col_peer(0, d) for d in (1, 2, 3)]
    peers += [row_peer(dx, dl, 0) for dx, dl in same_core] + [row_peer(0, 0, 1)]
    for peer in peers:
        pl.semaphore_signal(barrier, inc=1, device_id=peer, device_id_type=MESH)
    counts_in = []
    for n in range(4):
        at = pl.ds(n * SET, SET)
        counts_in.append(pltpu.make_async_copy(counts_hbm.at[at], counts.at[at], counts_sem))
        counts_in[-1].start()
    for copy in local:
        copy.wait()
    pl.semaphore_wait(barrier, len(peers))

    def give_rows(at, recv, to):
        remote(rows.at[at], rows.at[at], sent.at[0], recv, to).start()

    def give_cols(at, recv, to):
        remote(cols.at[at], cols.at[at], sent.at[1], recv, to).start()

    def wait_rows(count, recv):
        at = pl.ds(0, count)
        remote(rows.at[at], rows.at[at], sent.at[0], recv, col_peer(0, 1)).wait_recv()

    def wait_parts(count, recv):
        at = pl.ds(0, count * PART)
        remote(cols.at[at], cols.at[at], sent.at[1], recv, row_peer(0, 0, 1)).wait_recv()

    def send_cols(dx, dl):
        at = part_at(x * 4 + lax.rem(zl + dl, 2) * 2 + c)
        give_cols(at, gx_recv.at[2 * dx + dl - 1], row_peer(dx, 0, 0))

    give_cols(own_cols, gx_recv.at[0], row_peer(0, 1, 0))
    give_rows(own_rows, gz_recv.at[1], col_peer(1, 0))
    give_rows(own_rows, gz_recv.at[3], col_peer(3, 0))
    give_rows(own_rows, gf_recv, col_peer(0, 2))
    give_rows(own_rows, gs_recv.at[0], col_peer(0, 1))
    give_rows(own_rows, gs_recv.at[0], col_peer(0, 3))
    give_cols(own_cols, gc_recv.at[0], row_peer(0, 0, 1))
    for dx in (1, 3, 2):
        send_cols(dx, 0)
    give_rows(own_rows, gz_recv.at[2], col_peer(2, 0))

    row_logs = jnp.log(row_sums[...].astype(jnp.float32)) - log_total[0]
    for n in range(16):
        square = jnp.broadcast_to(row_logs[n : n + 1, :], (CHUNK, CHUNK))
        row_bias[n * CHUNK : (n + 1) * CHUNK, :] = square.T
    col_logs = jnp.log(col_sums[...].astype(jnp.float32))
    for t in range(4):
        both = [jnp.broadcast_to(col_logs[2 * t + h : 2 * t + h + 1, :], (8, CHUNK)) for h in (0, 1)]
        col_bias[t] = jnp.concatenate(both, axis=1)

    def forward_rows(d):
        wait_rows(CHUNK, gz_recv.at[d])
        for e in (1, 3) if d % 2 else (2, 1, 3):
            give_rows(chunk_at(lax.rem(zh + 4 - d, 4), y), gs_recv.at[d], col_peer(0, e))

    def forward_far():
        wait_rows(CHUNK, gf_recv)
        for d in (1, 3):
            give_rows(chunk_at(zh, lax.rem(y + 2, 4)), gs_recv.at[d], col_peer(d, 0))

    def forward_cols(n):
        dx, dl = same_core[n]
        wait_parts(1, gx_recv.at[n])
        at = part_at(lax.rem(x + 4 - dx, 4) * 4 + lax.rem(zl + dl, 2) * 2 + c)
        give_cols(at, gc_recv.at[dx], row_peer(0, 0, 1))
        if n == 0:
            for peer in (1, 3, 2):
                send_cols(peer, 1)

    def wait_cols(dx):
        wait_parts(2, gc_recv.at[dx])

    def wait_set(d):
        wait_rows((3 if d else 2) * CHUNK, gs_recv.at[d])

    def grads_of(at, tile, width):
        col_at = pl.ds(pl.multiple_of(tile * TILE, TILE), width)
        some = cols[col_at, :]
        scores = lax.dot_general(
            rows[at, :], some, (((1,), (1,)), ((), ())), preferred_element_type=jnp.float32
        )
        bias = jnp.concatenate([row_bias[at, :]] * (width // CHUNK), axis=1)
        side = jnp.concatenate([col_bias[tile + n, 0:1, :] for n in range(width // TILE)], axis=1)
        return cell_grads(counts[at, col_at], scores + bias + side, scale), some, col_at

    def tile_step(at, tile, width, first_rows, first_cols):
        grads, some, col_at = grads_of(at, tile, width)
        part = jnp.dot(grads, some, preferred_element_type=jnp.float32)
        row_total[...] = part if first_rows else row_total[...] + part
        part = lax.dot_general(
            grads, rows[at, :], (((0,), (0,)), ((), ())), preferred_element_type=jnp.float32
        )
        col_total[col_at, :] = part if first_cols else col_total[col_at, :] + part

    def set_at(d):
        return pl.ds(pl.multiple_of(lax.rem(zh + 4 - d, 4) * SET, SET), SET)

    slot_of = {1: 0, 3: 1, 2: 2}

    def y_message(d, e):
        n = slot_of[e]
        return remote(y_out.at[d, n], y_in.at[d, n], sent.at[2], ry_recv.at[d], col_peer(0, e))

    def far_message(d):
        return remote(y_out.at[d, 2], b_in.at[d // 2], sent.at[2], rb_recv, col_peer(4 - d, 0))

    def z_message(d):
        return remote(z_out.at[d - 1], z_in.at[d - 1], sent.at[3], rz_recv, col_peer(4 - d, 0))

    def peer_rows(e):
        return row_total[pl.ds(pl.multiple_of(lax.rem(y + e, 4) * CHUNK, CHUNK), CHUNK), :]

    def encode_rows(d):
        if d == 0:
            far[...] = peer_rows(2)
        else:
            encode(y_out.at[d, 2], peer_rows(2))
        encode(y_out.at[d, 0], peer_rows(1))
        encode(y_out.at[d, 1], peer_rows(3))
        kept[d] = peer_rows(0)

    def send_rows(d):
        if d % 2:
            far_message(d).start()
        elif d:
            y_message(d, 2).start()
        y_message(d, 1).start()
        y_message(d, 3).start()

    def send_far():
        remote(b_in, b_in, sent.at[2], rb_recv, col_peer(1, 0)).wait_recv()
        encode(y_out.at[0, 2], far[...] + decode(b_in.at[0], CHUNK) + decode(b_in.at[1], CHUNK))
        y_message(0, 2).start()

    def sum_rows(d):
        hops = 2 if d % 2 else 3
        arrived = y_in.at[d, pl.ds(0, hops)]
        remote(arrived, arrived, sent.at[2], ry_recv.at[d], col_peer(0, 1)).wait_recv()
        total = kept[d]
        for n in range(hops):
            total = total + decode(y_in.at[d, n], CHUNK)
        return total

    def send_z(d):
        encode(z_out.at[d - 1], sum_rows(d))
        z_message(d).start()

    odd, pair = x % 2, x // 2
    forward_cols(0)
    forward_rows(1)
    forward_rows(3)
    forward_far()
    for n in COLUMN_ORDER[1:4]:
        forward_cols(n)
    wait_set(0)
    pltpu.make_async_copy(counts_hbm, counts, counts_sem).wait()
    wait_cols(0)
    tile_step(set_at(0), x, TILE, True, True)
    for n in COLUMN_ORDER[4:]:
        forward_cols(n)
    wait_cols(3 - 2 * odd)
    tile_step(set_at(0), 2 * pair + 1 - odd, TILE, False, True)
    forward_rows(2)
    wait_cols(2)
    wait_cols(1 + 2 * odd)
    tile_step(set_at(0), 2 - 2 * pair, 2 * TILE, False, True)
    encode_rows(0)

    for d in SETS[:2]:
        wait_set(d)
        for tile in (0, 2):
            tile_step(set_at(d), tile, 2 * TILE, tile == 0, False)
        encode_rows(d)
        send_rows(d)
        if d == SETS[0]:
            send_rows(0)

    def core_message(n):
        return remote(c_out.at[n], c_in.at[n], sent.at[4], rc_recv.at[n], row_peer(0, 0, 1))

    def x_message(n):
        return remote(x_out.at[n], x_in.at[n], sent.at[5], rx_recv, row_peer(n + 1, 0, 0))

    def core_rows(n, h, core):
        return part_at(lax.rem(x + 1 + n, 4) * 4 + 2 * h + core)

    def send_core(n):
        theirs = [col_total[core_rows(n, h, 1 - c), :] for h in (0, 1)]
        encode(c_out.at[n], jnp.concatenate(theirs, axis=0))
        core_message(n).start()

    wait_set(SETS[2])
    tile_step(set_at(SETS[2]), 2 - 2 * pair, 2 * TILE, True, False)
    send_core(1)
    send_core(2 - 2 * odd)
    tile_step(set_at(SETS[2]), 2 * pair, 2 * TILE, False, False)
    encode_rows(SETS[2])
    send_rows(SETS[2])
    send_core(2 * odd)
    send_core(3)
    send_z(SETS[0])

    def both_cores(n):
        core_message(n).wait_recv()
        mine = [col_total[core_rows(n, h, c), :] for h in (0, 1)]
        return decode(c_in.at[n], 2 * PART) + jnp.concatenate(mine, axis=0)

    for n in (1, 2 - 2 * odd, 2 * odd):
        encode(x_out.at[n], both_cores(n))
        x_message(n).start()
    both = both_cores(3)

    send_z(SETS[1])
    send_z(SETS[2])
    send_far()
    remote(x_in, x_in, sent.at[5], rx_recv, row_peer(1, 0, 0)).wait_recv()
    for n in range(3):
        both = both + decode(x_in.at[n], 2 * PART)
    here = jnp.where(zl == 0, both[0:PART], both[PART:])
    encode(l_out, jnp.where(zl == 0, both[PART:], both[0:PART]))
    l_message = remote(l_out, l_in, sent.at[6], rl_recv, row_peer(0, 1, 0))
    l_message.start()
    row_sum = sum_rows(0)
    l_message.wait_recv()
    col_out[...] = here + decode(l_in, PART)

    for n, ref in (
        (0, rows.at[pl.ds(0, 15 * CHUNK)]), (1, cols.at[pl.ds(0, 15 * PART)]),
        (2, y_out), (3, z_out), (4, c_out), (5, x_out), (6, l_out),
    ):
        remote(ref, ref, sent.at[n], rl_recv, col_peer(0, 1)).wait_send()
    remote(z_in, z_in, sent.at[3], rz_recv, col_peer(1, 0)).wait_recv()
    for d in SETS:
        row_sum = row_sum + decode(z_in.at[d - 1], CHUNK)
    row_out[...] = row_sum


def shards(counts, row_sums, col_sums, log_total, row_emb, col_emb):
    n_cols = lax.axis_size("cols")
    scale = 1.0 / math.sqrt(col_sums.shape[0] * n_cols)
    dma = pltpu.SemaphoreType.DMA

    def body(*refs):
        kernel(scale, *refs)

    def hbm(array):
        return pltpu.with_memory_space_constraint(array, pltpu.HBM)

    anywhere = pl.BlockSpec(memory_space=pl.ANY)
    vmem = pl.BlockSpec(memory_space=pltpu.VMEM)
    message = (CHUNK + 16, D)
    return pl.pallas_call(
        body,
        name="swivel",
        out_shape=(
            jax.ShapeDtypeStruct((CHUNK, D), jnp.float32),
            jax.ShapeDtypeStruct((PART, D), jnp.float32),
        ),
        in_specs=[anywhere] * 3 + [pl.BlockSpec(memory_space=pltpu.SMEM)] + [anywhere] * 2,
        out_specs=(vmem, vmem),
        scratch_shapes=[
            pltpu.VMEM(counts.shape, jnp.int32),
            pltpu.VMEM((16, CHUNK), jnp.int32),
            pltpu.VMEM((8, CHUNK), jnp.int32),
            pltpu.VMEM((16 * CHUNK, D), jnp.bfloat16),
            pltpu.VMEM((16 * PART, D), jnp.bfloat16),
            pltpu.VMEM((16 * CHUNK, CHUNK), jnp.float32),
            pltpu.VMEM((4, 8, TILE), jnp.float32),
            pltpu.VMEM((4, CHUNK, D), jnp.float32),
            pltpu.VMEM((CHUNK, D), jnp.float32),
            pltpu.VMEM((SET, D), jnp.float32),
            pltpu.VMEM((16 * PART, D), jnp.float32),
            pltpu.VMEM((4, 3) + message, jnp.int16),
            pltpu.VMEM((4, 3) + message, jnp.int16),
            pltpu.VMEM((2,) + message, jnp.int16),
            pltpu.VMEM((3,) + message, jnp.int16),
            pltpu.VMEM((3,) + message, jnp.int16),
            pltpu.VMEM((4,) + message, jnp.int16),
            pltpu.VMEM((4,) + message, jnp.int16),
            pltpu.VMEM((3,) + message, jnp.int16),
            pltpu.VMEM((3,) + message, jnp.int16),
            pltpu.VMEM((PART + 16, D), jnp.int16),
            pltpu.VMEM((PART + 16, D), jnp.int16),
            dma((4,)), dma, dma((7,)),
            dma((4,)), dma((4,)), dma, dma((7,)), dma((4,)),
            dma((4,)), dma, dma, dma((4,)), dma, dma,
        ],
        compiler_params=pltpu.CompilerParams(
            collective_id=0, has_side_effects=True, vmem_limit_bytes=48 << 20
        ),
        cost_estimate=pl.CostEstimate(
            flops=6 * 2048 * 1024 * 256, bytes_accessed=9 << 20, transcendentals=3 * 2048 * 1024
        ),
    )(
        counts, hbm(row_sums.reshape(16, CHUNK)), hbm(col_sums.reshape(8, CHUNK)), log_total, hbm(row_emb), hbm(col_emb)
    )


def solution(mesh):
    in_specs = (
        P("rows", "cols"),
        P("rows"),
        P("cols"),
        P(),
        P(("rows", "cols"), None),
        P(("cols", "rows"), None),
    )
    out_specs = (P(("rows", "cols"), None), P(("cols", "rows"), None))
    return jax.shard_map(shards, mesh=mesh, in_specs=in_specs, out_specs=out_specs, check_vma=False)
```

```python
import math

import jax
import jax.numpy as jnp
from jax import lax
from jax.experimental import pallas as pl
from jax.experimental.pallas import tpu as pltpu
from jax.sharding import PartitionSpec as P

MESH = pl.DeviceIdType.MESH
D = 256
CHUNK = 128
PART = 64
SET = 4 * CHUNK
TILE = 4 * PART
LEVELS = 32000.0
STEPS = 8.0
COLUMN_ORDER = (0, 1, 5, 3, 2, 6, 4)
SETS = (1, 3, 2)


def encode(ref, value):
    rows = value.shape[0]
    top = jnp.max(jnp.abs(value), axis=0, keepdims=True)
    power = jnp.ceil(jnp.log(jnp.maximum(top, 1e-33)) * (STEPS / math.log(2.0)))
    inverse = jnp.exp(power * (-math.log(2.0) / STEPS)) * LEVELS
    ref[0:rows, :] = jnp.round(value * inverse).astype(jnp.int32).astype(jnp.int16)
    ref[rows : rows + 16, :] = (
        jnp.broadcast_to(power, (16, value.shape[1])).astype(jnp.int32).astype(jnp.int16)
    )


def decode(ref, rows):
    power = ref[rows : rows + 16, :].astype(jnp.int32).astype(jnp.float32)[0:1]
    scale = jnp.exp(power * (math.log(2.0) / STEPS)) * (1.0 / LEVELS)
    return ref[0:rows, :].astype(jnp.int32).astype(jnp.float32) * scale


def cell_grads(counts, scores, scale):
    at_least_one = jnp.maximum(counts.astype(jnp.float32), 1.0)
    root = at_least_one * lax.rsqrt(at_least_one)
    conf = (0.1 * scale) + (0.25 * scale) * root
    fitted = conf * (scores - jnp.log(at_least_one))
    hinge = (0.5 * scale) + (0.5 * scale) * jnp.tanh(0.5 * scores)
    return jnp.where(counts > 0, fitted, hinge).astype(jnp.bfloat16)


def kernel(
    scale,
    counts_hbm, row_sums_hbm, col_sums_hbm, log_total, row_emb, col_emb,
    row_out, col_out,
    counts, row_sums, col_sums, rows, cols, row_bias, col_bias,
    kept, far, row_total, col_total,
    y_out, y_in, b_in, z_out, z_in, c_out, c_in, x_out, x_in, l_out, l_in,
    local_sem, counts_sem, sent,
    gz_recv, gs_recv, gf_recv, gx_recv, gc_recv,
    ry_recv, rb_recv, rz_recv, rc_recv, rx_recv, rl_recv,
):
    r, k = lax.axis_index("rows"), lax.axis_index("cols")
    x, zl, c = r // 4, (r // 2) % 2, r % 2
    zh, y = k // 4, k % 4

    def col_peer(dz, dy):
        return (r, lax.rem(zh + dz, 4) * 4 + lax.rem(y + dy, 4))

    def row_peer(dx, dl, dc):
        return (lax.rem(x + dx, 4) * 4 + lax.rem(zl + dl, 2) * 2 + lax.rem(c + dc, 2), k)

    def chunk_at(z, yy):
        return pl.ds(pl.multiple_of((z * 4 + yy) * CHUNK, CHUNK), CHUNK)

    def part_at(index):
        return pl.ds(pl.multiple_of(index * PART, PART), PART)

    def remote(src, dst, send, recv, to):
        return pltpu.make_async_remote_copy(
            src_ref=src, dst_ref=dst, send_sem=send, recv_sem=recv, device_id=to, device_id_type=MESH
        )

    same_core = [(dx, dl) for dx in range(4) for dl in range(2) if dx or dl]

    own_rows, own_cols = chunk_at(zh, y), part_at(r)
    local = [
        pltpu.make_async_copy(row_emb, rows.at[own_rows], local_sem.at[0]),
        pltpu.make_async_copy(col_emb, cols.at[own_cols], local_sem.at[1]),
        pltpu.make_async_copy(row_sums_hbm, row_sums, local_sem.at[2]),
        pltpu.make_async_copy(col_sums_hbm, col_sums, local_sem.at[3]),
    ]
    for copy in local:
        copy.start()
    barrier = pltpu.get_barrier_semaphore()
    peers = [col_peer(d, 0) for d in (1, 2, 3)] + [col_peer(0, d) for d in (1, 2, 3)]
    peers += [row_peer(dx, dl, 0) for dx, dl in same_core] + [row_peer(0, 0, 1)]
    for peer in peers:
        pl.semaphore_signal(barrier, inc=1, device_id=peer, device_id_type=MESH)
    counts_in = []
    for n in range(4):
        at = pl.ds(n * SET, SET)
        counts_in.append(pltpu.make_async_copy(counts_hbm.at[at], counts.at[at], counts_sem))
        counts_in[-1].start()
    for copy in local:
        copy.wait()
    pl.semaphore_wait(barrier, len(peers))

    def give_rows(at, recv, to):
        remote(rows.at[at], rows.at[at], sent.at[0], recv, to).start()

    def give_cols(at, recv, to):
        remote(cols.at[at], cols.at[at], sent.at[1], recv, to).start()

    def wait_rows(count, recv):
        at = pl.ds(0, count)
        remote(rows.at[at], rows.at[at], sent.at[0], recv, col_peer(0, 1)).wait_recv()

    def wait_parts(count, recv):
        at = pl.ds(0, count * PART)
        remote(cols.at[at], cols.at[at], sent.at[1], recv, row_peer(0, 0, 1)).wait_recv()

    def send_cols(dx, dl):
        at = part_at(x * 4 + lax.rem(zl + dl, 2) * 2 + c)
        give_cols(at, gx_recv.at[2 * dx + dl - 1], row_peer(dx, 0, 0))

    give_cols(own_cols, gx_recv.at[0], row_peer(0, 1, 0))
    give_rows(own_rows, gz_recv.at[1], col_peer(1, 0))
    give_rows(own_rows, gz_recv.at[3], col_peer(3, 0))
    give_rows(own_rows, gf_recv, col_peer(0, 2))
    give_rows(own_rows, gs_recv.at[0], col_peer(0, 1))
    give_rows(own_rows, gs_recv.at[0], col_peer(0, 3))
    give_cols(own_cols, gc_recv.at[0], row_peer(0, 0, 1))
    for dx in (1, 3, 2):
        send_cols(dx, 0)
    give_rows(own_rows, gz_recv.at[2], col_peer(2, 0))

    row_logs = jnp.log(row_sums[...].astype(jnp.float32)) - log_total[0]
    for n in range(16):
        square = jnp.broadcast_to(row_logs[n : n + 1, :], (CHUNK, CHUNK))
        row_bias[n * CHUNK : (n + 1) * CHUNK, :] = square.T
    col_logs = jnp.log(col_sums[...].astype(jnp.float32))
    for t in range(4):
        both = [jnp.broadcast_to(col_logs[2 * t + h : 2 * t + h + 1, :], (8, CHUNK)) for h in (0, 1)]
        col_bias[t] = jnp.concatenate(both, axis=1)

    def forward_rows(d):
        wait_rows(CHUNK, gz_recv.at[d])
        for e in (1, 3) if d % 2 else (2, 1, 3):
            give_rows(chunk_at(lax.rem(zh + 4 - d, 4), y), gs_recv.at[d], col_peer(0, e))

    def forward_far():
        wait_rows(CHUNK, gf_recv)
        for d in (1, 3):
            give_rows(chunk_at(zh, lax.rem(y + 2, 4)), gs_recv.at[d], col_peer(d, 0))

    def forward_cols(n):
        dx, dl = same_core[n]
        wait_parts(1, gx_recv.at[n])
        at = part_at(lax.rem(x + 4 - dx, 4) * 4 + lax.rem(zl + dl, 2) * 2 + c)
        give_cols(at, gc_recv.at[dx], row_peer(0, 0, 1))
        if n == 0:
            for peer in (1, 3, 2):
                send_cols(peer, 1)

    def wait_cols(dx):
        wait_parts(2, gc_recv.at[dx])

    def wait_set(d):
        wait_rows((3 if d else 2) * CHUNK, gs_recv.at[d])

    def grads_of(at, tile, width):
        col_at = pl.ds(pl.multiple_of(tile * TILE, TILE), width)
        some = cols[col_at, :]
        scores = lax.dot_general(
            rows[at, :], some, (((1,), (1,)), ((), ())), preferred_element_type=jnp.float32
        )
        bias = jnp.concatenate([row_bias[at, :]] * (width // CHUNK), axis=1)
        side = jnp.concatenate([col_bias[tile + n, 0:1, :] for n in range(width // TILE)], axis=1)
        return cell_grads(counts[at, col_at], scores + bias + side, scale), some, col_at

    def tile_step(at, tile, width, first_rows, first_cols):
        grads, some, col_at = grads_of(at, tile, width)
        part = jnp.dot(grads, some, preferred_element_type=jnp.float32)
        row_total[...] = part if first_rows else row_total[...] + part
        part = lax.dot_general(
            grads, rows[at, :], (((0,), (0,)), ((), ())), preferred_element_type=jnp.float32
        )
        col_total[col_at, :] = part if first_cols else col_total[col_at, :] + part

    def half_step(d, hops):
        z = lax.rem(zh + 4 - d, 4)
        ats = [chunk_at(z, lax.rem(y + e, 4)) for e in hops]
        some = jnp.concatenate([rows[at, :] for at in ats], axis=0)
        scores = lax.dot_general(
            some, cols[...], (((1,), (1,)), ((), ())), preferred_element_type=jnp.float32
        )
        bias = jnp.concatenate([row_bias[at, :] for at in ats], axis=0)
        bias = jnp.concatenate([bias] * (4 * TILE // CHUNK), axis=1)
        side = jnp.concatenate([col_bias[n, 0:1, :] for n in range(4)], axis=1)
        found = jnp.concatenate([counts[at, :] for at in ats], axis=0)
        grads = cell_grads(found, scores + bias + side, scale)
        col_total[...] += lax.dot_general(
            grads, some, (((0,), (0,)), ((), ())), preferred_element_type=jnp.float32
        )
        return jnp.dot(grads, cols[...], preferred_element_type=jnp.float32)

    def set_at(d):
        return pl.ds(pl.multiple_of(lax.rem(zh + 4 - d, 4) * SET, SET), SET)

    slot_of = {1: 0, 3: 1, 2: 2}

    def y_message(d, e):
        n = slot_of[e]
        return remote(y_out.at[d, n], y_in.at[d, n], sent.at[2], ry_recv.at[d], col_peer(0, e))

    def far_message(d):
        return remote(y_out.at[d, 2], b_in.at[d // 2], sent.at[2], rb_recv, col_peer(4 - d, 0))

    def z_message(d):
        return remote(z_out.at[d - 1], z_in.at[d - 1], sent.at[3], rz_recv, col_peer(4 - d, 0))

    def peer_rows(e):
        return row_total[pl.ds(pl.multiple_of(lax.rem(y + e, 4) * CHUNK, CHUNK), CHUNK), :]

    def encode_rows(d):
        if d == 0:
            far[...] = peer_rows(2)
        else:
            encode(y_out.at[d, 2], peer_rows(2))
        encode(y_out.at[d, 0], peer_rows(1))
        encode(y_out.at[d, 1], peer_rows(3))
        kept[d] = peer_rows(0)

    def send_rows(d):
        if d % 2:
            far_message(d).start()
        elif d:
            y_message(d, 2).start()
        y_message(d, 1).start()
        y_message(d, 3).start()

    def send_far():
        remote(b_in, b_in, sent.at[2], rb_recv, col_peer(1, 0)).wait_recv()
        encode(y_out.at[0, 2], far[...] + decode(b_in.at[0], CHUNK) + decode(b_in.at[1], CHUNK))
        y_message(0, 2).start()

    def sum_rows(d):
        hops = 2 if d % 2 else 3
        arrived = y_in.at[d, pl.ds(0, hops)]
        remote(arrived, arrived, sent.at[2], ry_recv.at[d], col_peer(0, 1)).wait_recv()
        total = kept[d]
        for n in range(hops):
            total = total + decode(y_in.at[d, n], CHUNK)
        return total

    def send_z(d):
        encode(z_out.at[d - 1], sum_rows(d))
        z_message(d).start()

    odd, pair = x % 2, x // 2
    forward_cols(0)
    for n in COLUMN_ORDER[1:4]:
        forward_cols(n)
    forward_rows(1)
    forward_rows(3)
    forward_far()
    wait_set(0)
    pltpu.make_async_copy(counts_hbm, counts, counts_sem).wait()
    wait_cols(0)
    for n in COLUMN_ORDER[4:]:
        forward_cols(n)
    tile_step(set_at(0), x, TILE, True, True)
    wait_cols(3 - 2 * odd)
    tile_step(set_at(0), 2 * pair + 1 - odd, TILE, False, True)
    forward_rows(2)
    wait_cols(2)
    wait_cols(1 + 2 * odd)
    tile_step(set_at(0), 2 - 2 * pair, 2 * TILE, False, True)
    encode_rows(0)

    for d in SETS[:2]:
        wait_set(d)
        for tile in (0, 2):
            tile_step(set_at(d), tile, 2 * TILE, tile == 0, False)
        encode_rows(d)
        send_rows(d)

    def core_message(n):
        return remote(c_out.at[n], c_in.at[n], sent.at[4], rc_recv.at[n], row_peer(0, 0, 1))

    def x_message(n):
        return remote(x_out.at[n], x_in.at[n], sent.at[5], rx_recv, row_peer(n + 1, 0, 0))

    def core_rows(n, h, core):
        return part_at(lax.rem(x + 1 + n, 4) * 4 + 2 * h + core)

    def send_core(n):
        theirs = [col_total[core_rows(n, h, 1 - c), :] for h in (0, 1)]
        encode(c_out.at[n], jnp.concatenate(theirs, axis=0))
        core_message(n).start()

    wait_set(2)
    row_part = half_step(2, (2, 1))
    encode(y_out.at[2, 2], row_part[0:CHUNK])
    encode(y_out.at[2, 0], row_part[CHUNK:])
    y_message(2, 2).start()
    y_message(2, 1).start()
    row_part = half_step(2, (3, 0))
    encode(y_out.at[2, 1], row_part[0:CHUNK])
    y_message(2, 3).start()
    kept[2] = row_part[CHUNK:]
    for n in (1, 2 - 2 * odd, 2 * odd, 3):
        send_core(n)
    send_rows(0)
    send_z(SETS[0])

    def both_cores(n):
        core_message(n).wait_recv()
        mine = [col_total[core_rows(n, h, c), :] for h in (0, 1)]
        return decode(c_in.at[n], 2 * PART) + jnp.concatenate(mine, axis=0)

    for n in (1, 2 - 2 * odd, 2 * odd):
        encode(x_out.at[n], both_cores(n))
        x_message(n).start()
    both = both_cores(3)

    send_z(SETS[1])
    send_far()
    send_z(SETS[2])
    remote(x_in, x_in, sent.at[5], rx_recv, row_peer(1, 0, 0)).wait_recv()
    for n in range(3):
        both = both + decode(x_in.at[n], 2 * PART)
    here = jnp.where(zl == 0, both[0:PART], both[PART:])
    encode(l_out, jnp.where(zl == 0, both[PART:], both[0:PART]))
    l_message = remote(l_out, l_in, sent.at[6], rl_recv, row_peer(0, 1, 0))
    l_message.start()
    row_sum = sum_rows(0)
    l_message.wait_recv()
    col_out[...] = here + decode(l_in, PART)

    for n, ref in (
        (0, rows.at[pl.ds(0, 15 * CHUNK)]), (1, cols.at[pl.ds(0, 15 * PART)]),
        (2, y_out), (3, z_out), (4, c_out), (5, x_out), (6, l_out),
    ):
        remote(ref, ref, sent.at[n], rl_recv, col_peer(0, 1)).wait_send()
    remote(z_in, z_in, sent.at[3], rz_recv, col_peer(1, 0)).wait_recv()
    for d in SETS:
        row_sum = row_sum + decode(z_in.at[d - 1], CHUNK)
    row_out[...] = row_sum


def shards(counts, row_sums, col_sums, log_total, row_emb, col_emb):
    n_cols = lax.axis_size("cols")
    scale = 1.0 / math.sqrt(col_sums.shape[0] * n_cols)
    dma = pltpu.SemaphoreType.DMA

    def body(*refs):
        kernel(scale, *refs)

    def hbm(array):
        return pltpu.with_memory_space_constraint(array, pltpu.HBM)

    anywhere = pl.BlockSpec(memory_space=pl.ANY)
    vmem = pl.BlockSpec(memory_space=pltpu.VMEM)
    message = (CHUNK + 16, D)
    return pl.pallas_call(
        body,
        name="swivel",
        out_shape=(
            jax.ShapeDtypeStruct((CHUNK, D), jnp.float32),
            jax.ShapeDtypeStruct((PART, D), jnp.float32),
        ),
        in_specs=[anywhere] * 3 + [pl.BlockSpec(memory_space=pltpu.SMEM)] + [anywhere] * 2,
        out_specs=(vmem, vmem),
        scratch_shapes=[
            pltpu.VMEM(counts.shape, jnp.int32),
            pltpu.VMEM((16, CHUNK), jnp.int32),
            pltpu.VMEM((8, CHUNK), jnp.int32),
            pltpu.VMEM((16 * CHUNK, D), jnp.bfloat16),
            pltpu.VMEM((16 * PART, D), jnp.bfloat16),
            pltpu.VMEM((16 * CHUNK, CHUNK), jnp.float32),
            pltpu.VMEM((4, 8, TILE), jnp.float32),
            pltpu.VMEM((4, CHUNK, D), jnp.float32),
            pltpu.VMEM((CHUNK, D), jnp.float32),
            pltpu.VMEM((SET, D), jnp.float32),
            pltpu.VMEM((16 * PART, D), jnp.float32),
            pltpu.VMEM((4, 3) + message, jnp.int16),
            pltpu.VMEM((4, 3) + message, jnp.int16),
            pltpu.VMEM((2,) + message, jnp.int16),
            pltpu.VMEM((3,) + message, jnp.int16),
            pltpu.VMEM((3,) + message, jnp.int16),
            pltpu.VMEM((4,) + message, jnp.int16),
            pltpu.VMEM((4,) + message, jnp.int16),
            pltpu.VMEM((3,) + message, jnp.int16),
            pltpu.VMEM((3,) + message, jnp.int16),
            pltpu.VMEM((PART + 16, D), jnp.int16),
            pltpu.VMEM((PART + 16, D), jnp.int16),
            dma((4,)), dma, dma((7,)),
            dma((4,)), dma((4,)), dma, dma((7,)), dma((4,)),
            dma((4,)), dma, dma, dma((4,)), dma, dma,
        ],
        compiler_params=pltpu.CompilerParams(
            collective_id=0, has_side_effects=True, vmem_limit_bytes=48 << 20
        ),
        cost_estimate=pl.CostEstimate(
            flops=6 * 2048 * 1024 * 256, bytes_accessed=9 << 20, transcendentals=3 * 2048 * 1024
        ),
    )(
        counts, hbm(row_sums.reshape(16, CHUNK)), hbm(col_sums.reshape(8, CHUNK)), log_total, hbm(row_emb), hbm(col_emb)
    )


def solution(mesh):
    in_specs = (
        P("rows", "cols"),
        P("rows"),
        P("cols"),
        P(),
        P(("rows", "cols"), None),
        P(("cols", "rows"), None),
    )
    out_specs = (P(("rows", "cols"), None), P(("cols", "rows"), None))
    return jax.shard_map(shards, mesh=mesh, in_specs=in_specs, out_specs=out_specs, check_vma=False)
```

```python
import math

import jax
import jax.numpy as jnp
from jax import lax
from jax.experimental import pallas as pl
from jax.experimental.pallas import tpu as pltpu
from jax.sharding import PartitionSpec as P

MESH = pl.DeviceIdType.MESH
D = 256
CHUNK = 128
PART = 64
SET = 4 * CHUNK
TILE = 4 * PART
LEVELS = 32000.0
STEPS = 8.0
COLUMN_ORDER = (0, 1, 5, 3, 2, 6, 4)
SETS = (1, 3, 2)


def encode(ref, value):
    rows = value.shape[0]
    top = jnp.max(jnp.abs(value), axis=0, keepdims=True)
    power = jnp.ceil(jnp.log(jnp.maximum(top, 1e-33)) * (STEPS / math.log(2.0)))
    inverse = jnp.exp(power * (-math.log(2.0) / STEPS)) * LEVELS
    ref[0:rows, :] = jnp.round(value * inverse).astype(jnp.int32).astype(jnp.int16)
    ref[rows : rows + 16, :] = (
        jnp.broadcast_to(power, (16, value.shape[1])).astype(jnp.int32).astype(jnp.int16)
    )


def decode(ref, rows):
    power = ref[rows : rows + 16, :].astype(jnp.int32).astype(jnp.float32)[0:1]
    scale = jnp.exp(power * (math.log(2.0) / STEPS)) * (1.0 / LEVELS)
    return ref[0:rows, :].astype(jnp.int32).astype(jnp.float32) * scale


def of_counts(counts, scale):
    at_least_one = jnp.maximum(counts.astype(jnp.float32), 1.0)
    root = at_least_one * lax.rsqrt(at_least_one)
    conf = (0.1 * scale) + (0.25 * scale) * root
    return jnp.where(counts > 0, conf, -1.0), conf * jnp.log(at_least_one)


def cell_grads(conf, logs, scores, scale):
    fitted = conf * scores - logs
    hinge = (0.5 * scale) + (0.5 * scale) * jnp.tanh(0.5 * scores)
    return jnp.where(conf > 0, fitted, hinge).astype(jnp.bfloat16)


def kernel(
    scale,
    counts_hbm, row_sums_hbm, col_sums_hbm, log_total, row_emb, col_emb,
    row_out, col_out,
    counts, confs, count_logs, row_sums, col_sums, rows, cols, row_bias, col_bias,
    kept, far, row_total, col_total,
    y_out, y_in, b_in, z_out, z_in, c_out, c_in, x_out, x_in, l_out, l_in,
    local_sem, counts_sem, sent,
    gz_recv, gs_recv, gf_recv, gx_recv, gc_recv,
    ry_recv, rb_recv, rz_recv, rc_recv, rx_recv, rl_recv,
):
    r, k = lax.axis_index("rows"), lax.axis_index("cols")
    x, zl, c = r // 4, (r // 2) % 2, r % 2
    zh, y = k // 4, k % 4

    def col_peer(dz, dy):
        return (r, lax.rem(zh + dz, 4) * 4 + lax.rem(y + dy, 4))

    def row_peer(dx, dl, dc):
        return (lax.rem(x + dx, 4) * 4 + lax.rem(zl + dl, 2) * 2 + lax.rem(c + dc, 2), k)

    def chunk_at(z, yy):
        return pl.ds(pl.multiple_of((z * 4 + yy) * CHUNK, CHUNK), CHUNK)

    def part_at(index):
        return pl.ds(pl.multiple_of(index * PART, PART), PART)

    def remote(src, dst, send, recv, to):
        return pltpu.make_async_remote_copy(
            src_ref=src, dst_ref=dst, send_sem=send, recv_sem=recv, device_id=to, device_id_type=MESH
        )

    same_core = [(dx, dl) for dx in range(4) for dl in range(2) if dx or dl]

    own_rows, own_cols = chunk_at(zh, y), part_at(r)
    local = [
        pltpu.make_async_copy(row_emb, rows.at[own_rows], local_sem.at[0]),
        pltpu.make_async_copy(col_emb, cols.at[own_cols], local_sem.at[1]),
        pltpu.make_async_copy(row_sums_hbm, row_sums, local_sem.at[2]),
        pltpu.make_async_copy(col_sums_hbm, col_sums, local_sem.at[3]),
    ]
    for copy in local:
        copy.start()
    barrier = pltpu.get_barrier_semaphore()
    peers = [col_peer(d, 0) for d in (1, 2, 3)] + [col_peer(0, d) for d in (1, 2, 3)]
    peers += [row_peer(dx, dl, 0) for dx, dl in same_core] + [row_peer(0, 0, 1)]
    for peer in peers:
        pl.semaphore_signal(barrier, inc=1, device_id=peer, device_id_type=MESH)
    counts_in = []
    for n in range(4):
        at = pl.ds(n * SET, SET)
        counts_in.append(pltpu.make_async_copy(counts_hbm.at[at], counts.at[at], counts_sem))
        counts_in[-1].start()
    for copy in local:
        copy.wait()
    pl.semaphore_wait(barrier, len(peers))

    def give_rows(at, recv, to):
        remote(rows.at[at], rows.at[at], sent.at[0], recv, to).start()

    def give_cols(at, recv, to):
        remote(cols.at[at], cols.at[at], sent.at[1], recv, to).start()

    def wait_rows(count, recv):
        at = pl.ds(0, count)
        remote(rows.at[at], rows.at[at], sent.at[0], recv, col_peer(0, 1)).wait_recv()

    def wait_parts(count, recv):
        at = pl.ds(0, count * PART)
        remote(cols.at[at], cols.at[at], sent.at[1], recv, row_peer(0, 0, 1)).wait_recv()

    def send_cols(dx, dl):
        at = part_at(x * 4 + lax.rem(zl + dl, 2) * 2 + c)
        give_cols(at, gx_recv.at[2 * dx + dl - 1], row_peer(dx, 0, 0))

    give_cols(own_cols, gx_recv.at[0], row_peer(0, 1, 0))
    give_rows(own_rows, gz_recv.at[1], col_peer(1, 0))
    give_rows(own_rows, gz_recv.at[3], col_peer(3, 0))
    give_rows(own_rows, gf_recv, col_peer(0, 2))
    give_rows(own_rows, gs_recv.at[0], col_peer(0, 1))
    give_rows(own_rows, gs_recv.at[0], col_peer(0, 3))
    give_cols(own_cols, gc_recv.at[0], row_peer(0, 0, 1))
    for dx in (1, 3, 2):
        send_cols(dx, 0)
    give_rows(own_rows, gz_recv.at[2], col_peer(2, 0))

    row_logs = jnp.log(row_sums[...].astype(jnp.float32)) - log_total[0]
    for n in range(16):
        square = jnp.broadcast_to(row_logs[n : n + 1, :], (CHUNK, CHUNK))
        row_bias[n * CHUNK : (n + 1) * CHUNK, :] = square.T
    col_logs = jnp.log(col_sums[...].astype(jnp.float32))
    for t in range(4):
        both = [jnp.broadcast_to(col_logs[2 * t + h : 2 * t + h + 1, :], (8, CHUNK)) for h in (0, 1)]
        col_bias[t] = jnp.concatenate(both, axis=1)

    pltpu.make_async_copy(counts_hbm, counts, counts_sem).wait()

    def prepare(step, _):
        at = pl.ds(pl.multiple_of(lax.rem(zh * 4 + 4 + step, 16) * CHUNK, CHUNK), CHUNK)
        confs[at, :], count_logs[at, :] = of_counts(counts[at, :], scale)
        return 0

    lax.fori_loop(0, 12, prepare, 0)

    def forward_rows(d):
        wait_rows(CHUNK, gz_recv.at[d])
        for e in (1, 3) if d % 2 else (2, 1, 3):
            give_rows(chunk_at(lax.rem(zh + 4 - d, 4), y), gs_recv.at[d], col_peer(0, e))

    def forward_far():
        wait_rows(CHUNK, gf_recv)
        for d in (1, 3):
            give_rows(chunk_at(zh, lax.rem(y + 2, 4)), gs_recv.at[d], col_peer(d, 0))

    def forward_cols(n):
        dx, dl = same_core[n]
        wait_parts(1, gx_recv.at[n])
        at = part_at(lax.rem(x + 4 - dx, 4) * 4 + lax.rem(zl + dl, 2) * 2 + c)
        give_cols(at, gc_recv.at[dx], row_peer(0, 0, 1))
        if n == 0:
            for peer in (1, 3, 2):
                send_cols(peer, 1)

    def wait_cols(dx):
        wait_parts(2, gc_recv.at[dx])

    def wait_set(d):
        wait_rows((3 if d else 2) * CHUNK, gs_recv.at[d])

    def grads_of(at, tile, width, own):
        col_at = pl.ds(pl.multiple_of(tile * TILE, TILE), width)
        some = cols[col_at, :]
        scores = lax.dot_general(
            rows[at, :], some, (((1,), (1,)), ((), ())), preferred_element_type=jnp.float32
        )
        bias = jnp.concatenate([row_bias[at, :]] * (width // CHUNK), axis=1)
        side = jnp.concatenate([col_bias[tile + n, 0:1, :] for n in range(width // TILE)], axis=1)
        if own:
            conf, logs = of_counts(counts[at, col_at], scale)
        else:
            conf, logs = confs[at, col_at], count_logs[at, col_at]
        return cell_grads(conf, logs, scores + bias + side, scale), some, col_at

    def tile_step(at, tile, width, first_rows, first_cols):
        grads, some, col_at = grads_of(at, tile, width, first_cols)
        part = jnp.dot(grads, some, preferred_element_type=jnp.float32)
        row_total[...] = part if first_rows else row_total[...] + part
        part = lax.dot_general(
            grads, rows[at, :], (((0,), (0,)), ((), ())), preferred_element_type=jnp.float32
        )
        col_total[col_at, :] = part if first_cols else col_total[col_at, :] + part

    def half_step(d, hops):
        z = lax.rem(zh + 4 - d, 4)
        ats = [chunk_at(z, lax.rem(y + e, 4)) for e in hops]
        some = jnp.concatenate([rows[at, :] for at in ats], axis=0)
        scores = lax.dot_general(
            some, cols[...], (((1,), (1,)), ((), ())), preferred_element_type=jnp.float32
        )
        bias = jnp.concatenate([row_bias[at, :] for at in ats], axis=0)
        bias = jnp.concatenate([bias] * (4 * TILE // CHUNK), axis=1)
        side = jnp.concatenate([col_bias[n, 0:1, :] for n in range(4)], axis=1)
        conf = jnp.concatenate([confs[at, :] for at in ats], axis=0)
        logs = jnp.concatenate([count_logs[at, :] for at in ats], axis=0)
        grads = cell_grads(conf, logs, scores + bias + side, scale)
        col_total[...] += lax.dot_general(
            grads, some, (((0,), (0,)), ((), ())), preferred_element_type=jnp.float32
        )
        return jnp.dot(grads, cols[...], preferred_element_type=jnp.float32)

    def set_at(d):
        return pl.ds(pl.multiple_of(lax.rem(zh + 4 - d, 4) * SET, SET), SET)

    slot_of = {1: 0, 3: 1, 2: 2}

    def y_message(d, e):
        n = slot_of[e]
        return remote(y_out.at[d, n], y_in.at[d, n], sent.at[2], ry_recv.at[d], col_peer(0, e))

    def far_message(d):
        return remote(y_out.at[d, 2], b_in.at[d // 2], sent.at[2], rb_recv, col_peer(4 - d, 0))

    def z_message(d):
        return remote(z_out.at[d - 1], z_in.at[d - 1], sent.at[3], rz_recv, col_peer(4 - d, 0))

    def peer_rows(e):
        return row_total[pl.ds(pl.multiple_of(lax.rem(y + e, 4) * CHUNK, CHUNK), CHUNK), :]

    def encode_rows(d):
        if d == 0:
            far[...] = peer_rows(2)
        else:
            encode(y_out.at[d, 2], peer_rows(2))
        encode(y_out.at[d, 0], peer_rows(1))
        encode(y_out.at[d, 1], peer_rows(3))
        kept[d] = peer_rows(0)

    def send_rows(d):
        if d % 2:
            far_message(d).start()
        elif d:
            y_message(d, 2).start()
        y_message(d, 1).start()
        y_message(d, 3).start()

    def send_far():
        remote(b_in, b_in, sent.at[2], rb_recv, col_peer(1, 0)).wait_recv()
        encode(y_out.at[0, 2], far[...] + decode(b_in.at[0], CHUNK) + decode(b_in.at[1], CHUNK))
        y_message(0, 2).start()

    def sum_rows(d):
        hops = 2 if d % 2 else 3
        arrived = y_in.at[d, pl.ds(0, hops)]
        remote(arrived, arrived, sent.at[2], ry_recv.at[d], col_peer(0, 1)).wait_recv()
        total = kept[d]
        for n in range(hops):
            total = total + decode(y_in.at[d, n], CHUNK)
        return total

    def send_z(d):
        encode(z_out.at[d - 1], sum_rows(d))
        z_message(d).start()

    odd, pair = x % 2, x // 2
    forward_cols(0)
    for n in COLUMN_ORDER[1:4]:
        forward_cols(n)
    forward_rows(1)
    forward_rows(3)
    forward_far()
    wait_set(0)
    wait_cols(0)
    for n in COLUMN_ORDER[4:]:
        forward_cols(n)
    tile_step(set_at(0), x, TILE, True, True)
    wait_cols(3 - 2 * odd)
    tile_step(set_at(0), 2 * pair + 1 - odd, TILE, False, True)
    forward_rows(2)
    wait_cols(2)
    wait_cols(1 + 2 * odd)
    tile_step(set_at(0), 2 - 2 * pair, 2 * TILE, False, True)
    encode_rows(0)

    for d in SETS[:2]:
        wait_set(d)
        for tile in (0, 2):
            tile_step(set_at(d), tile, 2 * TILE, tile == 0, False)
        encode_rows(d)
        send_rows(d)

    def core_message(n):
        return remote(c_out.at[n], c_in.at[n], sent.at[4], rc_recv.at[n], row_peer(0, 0, 1))

    def x_message(n):
        return remote(x_out.at[n], x_in.at[n], sent.at[5], rx_recv, row_peer(n + 1, 0, 0))

    def core_rows(n, h, core):
        return part_at(lax.rem(x + 1 + n, 4) * 4 + 2 * h + core)

    def send_core(n):
        theirs = [col_total[core_rows(n, h, 1 - c), :] for h in (0, 1)]
        encode(c_out.at[n], jnp.concatenate(theirs, axis=0))
        core_message(n).start()

    wait_set(2)
    row_part = half_step(2, (2, 1))
    encode(y_out.at[2, 2], row_part[0:CHUNK])
    encode(y_out.at[2, 0], row_part[CHUNK:])
    y_message(2, 2).start()
    y_message(2, 1).start()
    row_part = half_step(2, (3, 0))
    encode(y_out.at[2, 1], row_part[0:CHUNK])
    y_message(2, 3).start()
    kept[2] = row_part[CHUNK:]
    for n in (1, 2 - 2 * odd, 2 * odd, 3):
        send_core(n)
    send_rows(0)
    send_z(SETS[0])

    def both_cores(n):
        core_message(n).wait_recv()
        mine = [col_total[core_rows(n, h, c), :] for h in (0, 1)]
        return decode(c_in.at[n], 2 * PART) + jnp.concatenate(mine, axis=0)

    for n in (1, 2 - 2 * odd, 2 * odd):
        encode(x_out.at[n], both_cores(n))
        x_message(n).start()
    both = both_cores(3)

    send_z(SETS[1])
    send_far()
    send_z(SETS[2])
    remote(x_in, x_in, sent.at[5], rx_recv, row_peer(1, 0, 0)).wait_recv()
    for n in range(3):
        both = both + decode(x_in.at[n], 2 * PART)
    here = jnp.where(zl == 0, both[0:PART], both[PART:])
    encode(l_out, jnp.where(zl == 0, both[PART:], both[0:PART]))
    l_message = remote(l_out, l_in, sent.at[6], rl_recv, row_peer(0, 1, 0))
    l_message.start()
    row_sum = sum_rows(0)
    l_message.wait_recv()
    col_out[...] = here + decode(l_in, PART)

    for n, ref in (
        (0, rows.at[pl.ds(0, 15 * CHUNK)]), (1, cols.at[pl.ds(0, 15 * PART)]),
        (2, y_out), (3, z_out), (4, c_out), (5, x_out), (6, l_out),
    ):
        remote(ref, ref, sent.at[n], rl_recv, col_peer(0, 1)).wait_send()
    remote(z_in, z_in, sent.at[3], rz_recv, col_peer(1, 0)).wait_recv()
    for d in SETS:
        row_sum = row_sum + decode(z_in.at[d - 1], CHUNK)
    row_out[...] = row_sum


def shards(counts, row_sums, col_sums, log_total, row_emb, col_emb):
    n_cols = lax.axis_size("cols")
    scale = 1.0 / math.sqrt(col_sums.shape[0] * n_cols)
    dma = pltpu.SemaphoreType.DMA

    def body(*refs):
        kernel(scale, *refs)

    def hbm(array):
        return pltpu.with_memory_space_constraint(array, pltpu.HBM)

    anywhere = pl.BlockSpec(memory_space=pl.ANY)
    vmem = pl.BlockSpec(memory_space=pltpu.VMEM)
    message = (CHUNK + 16, D)
    return pl.pallas_call(
        body,
        name="swivel",
        out_shape=(
            jax.ShapeDtypeStruct((CHUNK, D), jnp.float32),
            jax.ShapeDtypeStruct((PART, D), jnp.float32),
        ),
        in_specs=[anywhere] * 3 + [pl.BlockSpec(memory_space=pltpu.SMEM)] + [anywhere] * 2,
        out_specs=(vmem, vmem),
        scratch_shapes=[
            pltpu.VMEM(counts.shape, jnp.int32),
            pltpu.VMEM(counts.shape, jnp.float32),
            pltpu.VMEM(counts.shape, jnp.float32),
            pltpu.VMEM((16, CHUNK), jnp.int32),
            pltpu.VMEM((8, CHUNK), jnp.int32),
            pltpu.VMEM((16 * CHUNK, D), jnp.bfloat16),
            pltpu.VMEM((16 * PART, D), jnp.bfloat16),
            pltpu.VMEM((16 * CHUNK, CHUNK), jnp.float32),
            pltpu.VMEM((4, 8, TILE), jnp.float32),
            pltpu.VMEM((4, CHUNK, D), jnp.float32),
            pltpu.VMEM((CHUNK, D), jnp.float32),
            pltpu.VMEM((SET, D), jnp.float32),
            pltpu.VMEM((16 * PART, D), jnp.float32),
            pltpu.VMEM((4, 3) + message, jnp.int16),
            pltpu.VMEM((4, 3) + message, jnp.int16),
            pltpu.VMEM((2,) + message, jnp.int16),
            pltpu.VMEM((3,) + message, jnp.int16),
            pltpu.VMEM((3,) + message, jnp.int16),
            pltpu.VMEM((4,) + message, jnp.int16),
            pltpu.VMEM((4,) + message, jnp.int16),
            pltpu.VMEM((3,) + message, jnp.int16),
            pltpu.VMEM((3,) + message, jnp.int16),
            pltpu.VMEM((PART + 16, D), jnp.int16),
            pltpu.VMEM((PART + 16, D), jnp.int16),
            dma((4,)), dma, dma((7,)),
            dma((4,)), dma((4,)), dma, dma((7,)), dma((4,)),
            dma((4,)), dma, dma, dma((4,)), dma, dma,
        ],
        compiler_params=pltpu.CompilerParams(
            collective_id=0, has_side_effects=True, vmem_limit_bytes=48 << 20
        ),
        cost_estimate=pl.CostEstimate(
            flops=6 * 2048 * 1024 * 256, bytes_accessed=9 << 20, transcendentals=3 * 2048 * 1024
        ),
    )(
        counts, hbm(row_sums.reshape(16, CHUNK)), hbm(col_sums.reshape(8, CHUNK)), log_total, hbm(row_emb), hbm(col_emb)
    )


def solution(mesh):
    in_specs = (
        P("rows", "cols"),
        P("rows"),
        P("cols"),
        P(),
        P(("rows", "cols"), None),
        P(("cols", "rows"), None),
    )
    out_specs = (P(("rows", "cols"), None), P(("cols", "rows"), None))
    return jax.shard_map(shards, mesh=mesh, in_specs=in_specs, out_specs=out_specs, check_vma=False)
```

```python
import math

import jax
import jax.numpy as jnp
from jax import lax
from jax.experimental import pallas as pl
from jax.experimental.pallas import tpu as pltpu
from jax.sharding import PartitionSpec as P

MESH = pl.DeviceIdType.MESH
D = 256
CHUNK = 128
PART = 64
SET = 4 * CHUNK
TILE = 4 * PART
LEVELS = 32000.0
STEPS = 8.0
COLUMN_ORDER = (0, 1, 5, 3, 2, 6, 4)
SETS = (1, 3, 2)


def encode(ref, value):
    rows = value.shape[0]
    top = jnp.max(jnp.abs(value), axis=0, keepdims=True)
    power = jnp.ceil(jnp.log(jnp.maximum(top, 1e-33)) * (STEPS / math.log(2.0)))
    inverse = jnp.exp(power * (-math.log(2.0) / STEPS)) * LEVELS
    ref[0:rows, :] = jnp.round(value * inverse).astype(jnp.int32).astype(jnp.int16)
    ref[rows : rows + 16, :] = (
        jnp.broadcast_to(power, (16, value.shape[1])).astype(jnp.int32).astype(jnp.int16)
    )


def decode(ref, rows):
    power = ref[rows : rows + 16, :].astype(jnp.int32).astype(jnp.float32)[0:1]
    scale = jnp.exp(power * (math.log(2.0) / STEPS)) * (1.0 / LEVELS)
    return ref[0:rows, :].astype(jnp.int32).astype(jnp.float32) * scale


def of_counts(counts, scale):
    at_least_one = jnp.maximum(counts.astype(jnp.float32), 1.0)
    root = at_least_one * lax.rsqrt(at_least_one)
    conf = (0.1 * scale) + (0.25 * scale) * root
    return jnp.where(counts > 0, conf, -1.0), conf * jnp.log(at_least_one)


def cell_grads(conf, logs, scores, scale):
    fitted = conf * scores - logs
    hinge = (0.5 * scale) + (0.5 * scale) * jnp.tanh(0.5 * scores)
    return jnp.where(conf > 0, fitted, hinge).astype(jnp.bfloat16)


def kernel(
    scale,
    counts_hbm, row_sums_hbm, col_sums_hbm, log_total, row_emb, col_emb,
    row_out, col_out,
    counts, confs, count_logs, row_sums, col_sums, rows, cols, row_bias, col_bias,
    kept, far, row_total, col_total,
    y_out, y_in, b_in, z_out, z_in, c_out, c_in, x_out, x_in, l_out, l_in,
    local_sem, counts_sem, sent,
    gz_recv, gs_recv, gf_recv, gx_recv, gc_recv,
    ry_recv, rb_recv, rz_recv, rc_recv, rx_recv, rl_recv,
):
    r, k = lax.axis_index("rows"), lax.axis_index("cols")
    x, zl, c = r // 4, (r // 2) % 2, r % 2
    zh, y = k // 4, k % 4

    def col_peer(dz, dy):
        return (r, lax.rem(zh + dz, 4) * 4 + lax.rem(y + dy, 4))

    def row_peer(dx, dl, dc):
        return (lax.rem(x + dx, 4) * 4 + lax.rem(zl + dl, 2) * 2 + lax.rem(c + dc, 2), k)

    def chunk_at(z, yy):
        return pl.ds(pl.multiple_of((z * 4 + yy) * CHUNK, CHUNK), CHUNK)

    def part_at(index):
        return pl.ds(pl.multiple_of(index * PART, PART), PART)

    def remote(src, dst, send, recv, to):
        return pltpu.make_async_remote_copy(
            src_ref=src, dst_ref=dst, send_sem=send, recv_sem=recv, device_id=to, device_id_type=MESH
        )

    same_core = [(dx, dl) for dx in range(4) for dl in range(2) if dx or dl]

    own_rows, own_cols = chunk_at(zh, y), part_at(r)
    local = [
        pltpu.make_async_copy(row_emb, rows.at[own_rows], local_sem.at[0]),
        pltpu.make_async_copy(col_emb, cols.at[own_cols], local_sem.at[1]),
        pltpu.make_async_copy(row_sums_hbm, row_sums, local_sem.at[2]),
        pltpu.make_async_copy(col_sums_hbm, col_sums, local_sem.at[3]),
    ]
    for copy in local:
        copy.start()
    barrier = pltpu.get_barrier_semaphore()
    peers = [col_peer(d, 0) for d in (1, 2, 3)] + [col_peer(0, d) for d in (1, 2, 3)]
    peers += [row_peer(dx, dl, 0) for dx, dl in same_core] + [row_peer(0, 0, 1)]
    for peer in peers:
        pl.semaphore_signal(barrier, inc=1, device_id=peer, device_id_type=MESH)
    counts_in = []
    for n in range(4):
        at = pl.ds(n * SET, SET)
        counts_in.append(pltpu.make_async_copy(counts_hbm.at[at], counts.at[at], counts_sem))
        counts_in[-1].start()
    for copy in local:
        copy.wait()
    pl.semaphore_wait(barrier, len(peers))

    def give_rows(at, recv, to):
        remote(rows.at[at], rows.at[at], sent.at[0], recv, to).start()

    def give_cols(at, recv, to):
        remote(cols.at[at], cols.at[at], sent.at[1], recv, to).start()

    def wait_rows(count, recv):
        at = pl.ds(0, count)
        remote(rows.at[at], rows.at[at], sent.at[0], recv, col_peer(0, 1)).wait_recv()

    def wait_parts(count, recv):
        at = pl.ds(0, count * PART)
        remote(cols.at[at], cols.at[at], sent.at[1], recv, row_peer(0, 0, 1)).wait_recv()

    def send_cols(dx, dl):
        at = part_at(x * 4 + lax.rem(zl + dl, 2) * 2 + c)
        give_cols(at, gx_recv.at[2 * dx + dl - 1], row_peer(dx, 0, 0))

    give_cols(own_cols, gx_recv.at[0], row_peer(0, 1, 0))
    give_rows(own_rows, gz_recv.at[1], col_peer(1, 0))
    give_rows(own_rows, gz_recv.at[3], col_peer(3, 0))
    give_rows(own_rows, gf_recv, col_peer(0, 2))
    give_rows(own_rows, gs_recv.at[0], col_peer(0, 1))
    give_rows(own_rows, gs_recv.at[0], col_peer(0, 3))
    give_cols(own_cols, gc_recv.at[0], row_peer(0, 0, 1))
    for dx in (1, 3, 2):
        send_cols(dx, 0)
    give_rows(own_rows, gz_recv.at[2], col_peer(2, 0))

    row_logs = jnp.log(row_sums[...].astype(jnp.float32)) - log_total[0]
    for n in range(16):
        square = jnp.broadcast_to(row_logs[n : n + 1, :], (CHUNK, CHUNK))
        row_bias[n * CHUNK : (n + 1) * CHUNK, :] = square.T
    col_logs = jnp.log(col_sums[...].astype(jnp.float32))
    for t in range(4):
        both = [jnp.broadcast_to(col_logs[2 * t + h : 2 * t + h + 1, :], (8, CHUNK)) for h in (0, 1)]
        col_bias[t] = jnp.concatenate(both, axis=1)

    pltpu.make_async_copy(counts_hbm, counts, counts_sem).wait()

    def prepare(step, _):
        at = pl.ds(pl.multiple_of(lax.rem(zh * 4 + 4 + step, 16) * CHUNK, CHUNK), CHUNK)
        confs[at, :], count_logs[at, :] = of_counts(counts[at, :], scale)
        return 0

    lax.fori_loop(0, 12, prepare, 0)

    def forward_rows(d):
        wait_rows(CHUNK, gz_recv.at[d])
        for e in (1, 3) if d % 2 else (2, 1, 3):
            give_rows(chunk_at(lax.rem(zh + 4 - d, 4), y), gs_recv.at[d], col_peer(0, e))

    def forward_far():
        wait_rows(CHUNK, gf_recv)
        for d in (1, 3):
            give_rows(chunk_at(zh, lax.rem(y + 2, 4)), gs_recv.at[d], col_peer(d, 0))

    def forward_cols(n):
        dx, dl = same_core[n]
        wait_parts(1, gx_recv.at[n])
        at = part_at(lax.rem(x + 4 - dx, 4) * 4 + lax.rem(zl + dl, 2) * 2 + c)
        give_cols(at, gc_recv.at[dx], row_peer(0, 0, 1))
        if n == 0:
            for peer in (1, 3, 2):
                send_cols(peer, 1)

    def wait_cols(dx):
        wait_parts(2, gc_recv.at[dx])

    def wait_set(d):
        wait_rows((3 if d else 2) * CHUNK, gs_recv.at[d])

    def grads_of(at, tile, width, own):
        col_at = pl.ds(pl.multiple_of(tile * TILE, TILE), width)
        some = cols[col_at, :]
        scores = lax.dot_general(
            rows[at, :], some, (((1,), (1,)), ((), ())), preferred_element_type=jnp.float32
        )
        bias = jnp.concatenate([row_bias[at, :]] * (width // CHUNK), axis=1)
        side = jnp.concatenate([col_bias[tile + n, 0:1, :] for n in range(width // TILE)], axis=1)
        if own:
            conf, logs = of_counts(counts[at, col_at], scale)
        else:
            conf, logs = confs[at, col_at], count_logs[at, col_at]
        return cell_grads(conf, logs, scores + bias + side, scale), some, col_at

    def tile_step(at, tile, width, first_rows, first_cols):
        grads, some, col_at = grads_of(at, tile, width, first_cols)
        part = jnp.dot(grads, some, preferred_element_type=jnp.float32)
        row_total[...] = part if first_rows else row_total[...] + part
        part = lax.dot_general(
            grads, rows[at, :], (((0,), (0,)), ((), ())), preferred_element_type=jnp.float32
        )
        col_total[col_at, :] = part if first_cols else col_total[col_at, :] + part

    def half_step(d, hops):
        z = lax.rem(zh + 4 - d, 4)
        ats = [chunk_at(z, lax.rem(y + e, 4)) for e in hops]
        some = jnp.concatenate([rows[at, :] for at in ats], axis=0)
        scores = lax.dot_general(
            some, cols[...], (((1,), (1,)), ((), ())), preferred_element_type=jnp.float32
        )
        bias = jnp.concatenate([row_bias[at, :] for at in ats], axis=0)
        bias = jnp.concatenate([bias] * (4 * TILE // CHUNK), axis=1)
        side = jnp.concatenate([col_bias[n, 0:1, :] for n in range(4)], axis=1)
        conf = jnp.concatenate([confs[at, :] for at in ats], axis=0)
        logs = jnp.concatenate([count_logs[at, :] for at in ats], axis=0)
        grads = cell_grads(conf, logs, scores + bias + side, scale)
        col_total[...] += lax.dot_general(
            grads, some, (((0,), (0,)), ((), ())), preferred_element_type=jnp.float32
        )
        return jnp.dot(grads, cols[...], preferred_element_type=jnp.float32)

    def set_at(d):
        return pl.ds(pl.multiple_of(lax.rem(zh + 4 - d, 4) * SET, SET), SET)

    slot_of = {1: 0, 3: 1, 2: 2}

    def y_message(d, e):
        n = slot_of[e]
        return remote(y_out.at[d, n], y_in.at[d, n], sent.at[2], ry_recv.at[d], col_peer(0, e))

    def far_message(d):
        return remote(y_out.at[d, 2], b_in.at[d // 2], sent.at[2], rb_recv, col_peer(4 - d, 0))

    def z_message(d):
        return remote(z_out.at[d - 1], z_in.at[d - 1], sent.at[3], rz_recv, col_peer(4 - d, 0))

    def peer_rows(e):
        return row_total[pl.ds(pl.multiple_of(lax.rem(y + e, 4) * CHUNK, CHUNK), CHUNK), :]

    def encode_rows(d):
        if d == 0:
            far[...] = peer_rows(2)
        else:
            encode(y_out.at[d, 2], peer_rows(2))
        encode(y_out.at[d, 0], peer_rows(1))
        encode(y_out.at[d, 1], peer_rows(3))
        kept[d] = peer_rows(0)

    def send_rows(d):
        if d % 2:
            far_message(d).start()
        elif d:
            y_message(d, 2).start()
        y_message(d, 1).start()
        y_message(d, 3).start()

    def send_far():
        remote(b_in, b_in, sent.at[2], rb_recv, col_peer(1, 0)).wait_recv()
        encode(y_out.at[0, 2], far[...] + decode(b_in.at[0], CHUNK) + decode(b_in.at[1], CHUNK))
        y_message(0, 2).start()

    def sum_rows(d):
        hops = 2 if d % 2 else 3
        arrived = y_in.at[d, pl.ds(0, hops)]
        remote(arrived, arrived, sent.at[2], ry_recv.at[d], col_peer(0, 1)).wait_recv()
        total = kept[d]
        for n in range(hops):
            total = total + decode(y_in.at[d, n], CHUNK)
        return total

    def send_z(d):
        encode(z_out.at[d - 1], sum_rows(d))
        z_message(d).start()

    odd, pair = x % 2, x // 2
    forward_cols(0)
    for n in COLUMN_ORDER[1:4]:
        forward_cols(n)
    forward_rows(1)
    forward_rows(3)
    forward_far()
    wait_set(0)
    wait_cols(0)
    for n in COLUMN_ORDER[4:]:
        forward_cols(n)
    tile_step(set_at(0), x, TILE, True, True)
    wait_cols(3 - 2 * odd)
    tile_step(set_at(0), 2 * pair + 1 - odd, TILE, False, True)
    forward_rows(2)
    wait_cols(2)
    wait_cols(1 + 2 * odd)
    tile_step(set_at(0), 2 - 2 * pair, 2 * TILE, False, True)
    encode_rows(0)

    wait_set(1)
    for tile in (0, 2):
        tile_step(set_at(1), tile, 2 * TILE, tile == 0, False)
    encode_rows(1)
    send_rows(1)
    wait_set(3)
    row_part = half_step(3, (2, 1))
    encode(y_out.at[3, 2], row_part[0:CHUNK])
    encode(y_out.at[3, 0], row_part[CHUNK:])
    far_message(3).start()
    y_message(3, 1).start()
    row_part = half_step(3, (3, 0))
    encode(y_out.at[3, 1], row_part[0:CHUNK])
    y_message(3, 3).start()
    kept[3] = row_part[CHUNK:]

    def core_message(n):
        return remote(c_out.at[n], c_in.at[n], sent.at[4], rc_recv.at[n], row_peer(0, 0, 1))

    def x_message(n):
        return remote(x_out.at[n], x_in.at[n], sent.at[5], rx_recv, row_peer(n + 1, 0, 0))

    def core_rows(n, h, core):
        return part_at(lax.rem(x + 1 + n, 4) * 4 + 2 * h + core)

    def send_core(n):
        theirs = [col_total[core_rows(n, h, 1 - c), :] for h in (0, 1)]
        encode(c_out.at[n], jnp.concatenate(theirs, axis=0))
        core_message(n).start()

    wait_set(2)
    row_part = half_step(2, (2, 1))
    encode(y_out.at[2, 2], row_part[0:CHUNK])
    encode(y_out.at[2, 0], row_part[CHUNK:])
    y_message(2, 2).start()
    y_message(2, 1).start()
    row_part = half_step(2, (3, 0))
    encode(y_out.at[2, 1], row_part[0:CHUNK])
    y_message(2, 3).start()
    kept[2] = row_part[CHUNK:]
    for n in (1, 2 - 2 * odd, 2 * odd, 3):
        send_core(n)
    send_z(SETS[0])

    def both_cores(n):
        core_message(n).wait_recv()
        mine = [col_total[core_rows(n, h, c), :] for h in (0, 1)]
        return decode(c_in.at[n], 2 * PART) + jnp.concatenate(mine, axis=0)

    for n in (1, 2 - 2 * odd, 2 * odd):
        encode(x_out.at[n], both_cores(n))
        x_message(n).start()
    both = both_cores(3)

    send_z(SETS[1])
    send_rows(0)
    send_far()
    send_z(SETS[2])
    remote(x_in, x_in, sent.at[5], rx_recv, row_peer(1, 0, 0)).wait_recv()
    for n in range(3):
        both = both + decode(x_in.at[n], 2 * PART)
    here = jnp.where(zl == 0, both[0:PART], both[PART:])
    encode(l_out, jnp.where(zl == 0, both[PART:], both[0:PART]))
    l_message = remote(l_out, l_in, sent.at[6], rl_recv, row_peer(0, 1, 0))
    l_message.start()
    row_sum = sum_rows(0)
    l_message.wait_recv()
    col_out[...] = here + decode(l_in, PART)

    for n, ref in (
        (0, rows.at[pl.ds(0, 15 * CHUNK)]), (1, cols.at[pl.ds(0, 15 * PART)]),
        (2, y_out), (3, z_out), (4, c_out), (5, x_out), (6, l_out),
    ):
        remote(ref, ref, sent.at[n], rl_recv, col_peer(0, 1)).wait_send()
    remote(z_in, z_in, sent.at[3], rz_recv, col_peer(1, 0)).wait_recv()
    for d in SETS:
        row_sum = row_sum + decode(z_in.at[d - 1], CHUNK)
    row_out[...] = row_sum


def shards(counts, row_sums, col_sums, log_total, row_emb, col_emb):
    n_cols = lax.axis_size("cols")
    scale = 1.0 / math.sqrt(col_sums.shape[0] * n_cols)
    dma = pltpu.SemaphoreType.DMA

    def body(*refs):
        kernel(scale, *refs)

    def hbm(array):
        return pltpu.with_memory_space_constraint(array, pltpu.HBM)

    anywhere = pl.BlockSpec(memory_space=pl.ANY)
    vmem = pl.BlockSpec(memory_space=pltpu.VMEM)
    message = (CHUNK + 16, D)
    return pl.pallas_call(
        body,
        name="swivel",
        out_shape=(
            jax.ShapeDtypeStruct((CHUNK, D), jnp.float32),
            jax.ShapeDtypeStruct((PART, D), jnp.float32),
        ),
        in_specs=[anywhere] * 3 + [pl.BlockSpec(memory_space=pltpu.SMEM)] + [anywhere] * 2,
        out_specs=(vmem, vmem),
        scratch_shapes=[
            pltpu.VMEM(counts.shape, jnp.int32),
            pltpu.VMEM(counts.shape, jnp.float32),
            pltpu.VMEM(counts.shape, jnp.float32),
            pltpu.VMEM((16, CHUNK), jnp.int32),
            pltpu.VMEM((8, CHUNK), jnp.int32),
            pltpu.VMEM((16 * CHUNK, D), jnp.bfloat16),
            pltpu.VMEM((16 * PART, D), jnp.bfloat16),
            pltpu.VMEM((16 * CHUNK, CHUNK), jnp.float32),
            pltpu.VMEM((4, 8, TILE), jnp.float32),
            pltpu.VMEM((4, CHUNK, D), jnp.float32),
            pltpu.VMEM((CHUNK, D), jnp.float32),
            pltpu.VMEM((SET, D), jnp.float32),
            pltpu.VMEM((16 * PART, D), jnp.float32),
            pltpu.VMEM((4, 3) + message, jnp.int16),
            pltpu.VMEM((4, 3) + message, jnp.int16),
            pltpu.VMEM((2,) + message, jnp.int16),
            pltpu.VMEM((3,) + message, jnp.int16),
            pltpu.VMEM((3,) + message, jnp.int16),
            pltpu.VMEM((4,) + message, jnp.int16),
            pltpu.VMEM((4,) + message, jnp.int16),
            pltpu.VMEM((3,) + message, jnp.int16),
            pltpu.VMEM((3,) + message, jnp.int16),
            pltpu.VMEM((PART + 16, D), jnp.int16),
            pltpu.VMEM((PART + 16, D), jnp.int16),
            dma((4,)), dma, dma((7,)),
            dma((4,)), dma((4,)), dma, dma((7,)), dma((4,)),
            dma((4,)), dma, dma, dma((4,)), dma, dma,
        ],
        compiler_params=pltpu.CompilerParams(
            collective_id=0, has_side_effects=True, vmem_limit_bytes=48 << 20
        ),
        cost_estimate=pl.CostEstimate(
            flops=6 * 2048 * 1024 * 256, bytes_accessed=9 << 20, transcendentals=3 * 2048 * 1024
        ),
    )(
        counts, hbm(row_sums.reshape(16, CHUNK)), hbm(col_sums.reshape(8, CHUNK)), log_total, hbm(row_emb), hbm(col_emb)
    )


def solution(mesh):
    in_specs = (
        P("rows", "cols"),
        P("rows"),
        P("cols"),
        P(),
        P(("rows", "cols"), None),
        P(("cols", "rows"), None),
    )
    out_specs = (P(("rows", "cols"), None), P(("cols", "rows"), None))
    return jax.shard_map(shards, mesh=mesh, in_specs=in_specs, out_specs=out_specs, check_vma=False)
```
